512 devices in a mesh: expert: 8 (over z_lo, core), dp: 64 (over z_hi, x, y).
Axes of the slice: x: 4, y: 4, z: 16 (z_hi: 4, z_lo: 4; z = z_hi * 4 + z_lo), core: 2. Of those that a mesh axis runs over, the one named last changes fastest.
Arguments:
- x_rows: bfloat16 [8, 64, 8, 2, 3072], P('expert', 'dp'), may hold values from -6 to 6
- cot_rows: bfloat16 [8, 64, 8, 2, 3072], P('expert', 'dp'), may hold values from -3 to 3
- counts: int32 [8, 64, 8], P(None, 'dp'), may hold values from 0 to 2, as said below
- w_gate: bfloat16 [8, 3072, 8192], P('expert', None, 'dp'), may hold values from -0.109375 to 0.109375
- w_up: bfloat16 [8, 3072, 8192], P('expert', None, 'dp'), may hold values from -0.109375 to 0.109375
- w_down: bfloat16 [8, 8192, 3072], P('expert', 'dp'), may hold values from -0.0625 to 0.0625
- kept_blocks: int32 [8], P('expert'), may hold values from 16 to 64
- block_rank: int32 [8, 64], P('expert', 'dp'), may hold values from 0 to 63, each once within a row
Outputs:
- grad_rows: bfloat16 [8, 64, 8, 2, 3072], P('expert', 'dp')
- grad_gate: bfloat16 [8, 3072, 8192], P('expert', None, 'dp')
- grad_up: bfloat16 [8, 3072, 8192], P('expert', None, 'dp')
- grad_down: bfloat16 [8, 8192, 3072], P('expert', 'dp')
The draws below stay inside these ranges and needn't reach their ends.
Inputs may be any that keep to these rules, and one draw needn't show every extreme that they name: The live slots of a source's buffer for an expert are its first ones. For every expert e and index d the sum over sources s of counts[s, d, e] is at most 4, and it equals 4 for every d of some expert.
All inputs are finite; a program needn't handle non-finite values.
Results may differ from the reference program's by a relative error of at most 0.005.
Values may be sent and summed in bfloat16 or wider, within the bound.
No kernel may reach another device: no remote copies, remote signals or barrier semaphores. Data moves between devices by JAX's collectives and lax.ppermute only.
A program may use at most 64 MiB of HBM per device.

```python
import jax
import jax.numpy as jnp

D = 3072
BLOCK = 128
CAP = 2
LIVE = 4
EXPERTS = 8
HIDDEN_SIZE = 8192
N_EXPERT = 8
N_DP = 64


def draw_counts(key, part):
    key = jax.random.fold_in(key, 11)
    key_heavy, key_light, key_order = jax.random.split(key, 3)
    heavy = jax.random.randint(key_heavy, (), 0, EXPERTS)
    light = jax.random.randint(key_light, (EXPERTS, N_DP), 3 * LIVE // 4, LIVE + 1)
    chosen = jnp.arange(EXPERTS)[:, None] == heavy
    load = jnp.where(chosen, LIVE, light)
    scores = jax.random.randint(key_order, (EXPERTS, N_DP, N_EXPERT), 0, 1 << 20) * N_EXPERT + jnp.arange(N_EXPERT)
    order = jnp.argsort(jnp.argsort(scores, axis=-1), axis=-1)
    share = jnp.clip(load[:, :, None] - CAP * order, 0, CAP)
    return jnp.transpose(share, (2, 1, 0)).astype(jnp.int32)


def plant(array, rng, smallest, high):
    longest = array.shape.index(max(array.shape))
    spots = []
    for shift in (0, 1):
        where = [jax.random.randint(jax.random.fold_in(rng, axis), (), 0, length) for axis, length in enumerate(array.shape)]
        where[longest] = (where[longest] + shift) % array.shape[longest]
        spots.append(tuple(where))
    return array.at[spots[0]].set(smallest).at[spots[1]].set(high)


def block_scale(key, dims, shards, smallest, top_value):
    level, own = 1.0, jax.random.fold_in(key, 6)
    for dim, parts in shards:
        heights = jnp.exp(jax.random.uniform(jax.random.fold_in(own, dim), (parts,), jnp.float32, smallest / len(shards), top_value / len(shards)))
        level = level * jnp.repeat(heights, dims[dim] // parts).reshape([-1 if axis == dim else 1 for axis in range(len(dims))])
    return level


def bell_draw(own_key, shape, width, reach, shards=(), kind=jnp.bfloat16):
    entries = jax.random.normal(own_key, shape, jnp.float32) * width
    if len(shards) > 0:
        entries = block_scale(own_key, shape, shards, -0.22, 0.18) * entries
    return jnp.clip(entries, min=-reach, max=reach).astype(kind)


def setup_inputs(seed: int = 0) -> dict:
    key_list = jax.random.split(jax.random.key(seed), 9)
    x_rows = bell_draw(key_list[0], (N_EXPERT, N_DP, EXPERTS, CAP, D), 1.0, 6.0, ((0, 8), (1, 64)))
    cot_rows = bell_draw(key_list[1], (N_EXPERT, N_DP, EXPERTS, CAP, D), 0.5, 3.0, ((0, 8), (1, 64)))
    counts = draw_counts(jax.random.fold_in(key_list[8], 71), 0)
    w_gate = bell_draw(key_list[3], (EXPERTS, D, HIDDEN_SIZE), D ** -0.5, 0.109375, ((0, 8), (2, 64)))
    w_up = bell_draw(key_list[4], (EXPERTS, D, HIDDEN_SIZE), D ** -0.5, 0.109375, ((0, 8), (2, 64)))
    w_down = bell_draw(key_list[5], (EXPERTS, HIDDEN_SIZE, D), HIDDEN_SIZE ** -0.5, 0.0625, ((0, 8), (1, 64)))
    kept_blocks = plant(jax.random.randint(key_list[6], (EXPERTS,), N_DP // 4, N_DP + 1), jax.random.fold_in(key_list[6], 1), N_DP // 4, N_DP).astype(jnp.int32)
    block_rank = jax.vmap(lambda own: jax.random.permutation(own, N_DP))(jax.random.split(key_list[7], EXPERTS)).reshape((EXPERTS, N_DP)).astype(jnp.int32)
    return dict(x_rows=x_rows, cot_rows=cot_rows, counts=counts, w_gate=w_gate, w_up=w_up, w_down=w_down, kept_blocks=kept_blocks, block_rank=block_rank)


def compact_matrix(slot_counts, live_rows, capacity):
    sources = slot_counts.shape[0]
    within_slot = jnp.tile(jnp.arange(capacity, dtype=jnp.int32), sources)
    count_slot = jnp.repeat(slot_counts, capacity)
    offsets = jnp.repeat(jnp.cumsum(slot_counts) - slot_counts, capacity)
    target = offsets + within_slot
    alive = within_slot < count_slot
    row_index = jnp.arange(live_rows, dtype=jnp.int32)[:, None]
    return ((row_index == target[None, :]) & alive[None, :]).astype(jnp.bfloat16)


def pack_for(slot_counts):
    return compact_matrix(slot_counts, LIVE, CAP)


def reference(x_rows, cot_rows, counts, w_gate, w_up, w_down, kept_blocks, block_rank):
    row_parts = []
    gate_parts = []
    up_parts = []
    down_parts = []
    for expert_id in range(EXPERTS):
        chooser = jax.vmap(pack_for)(jnp.transpose(counts[:, :, expert_id], (1, 0)))
        chooser_f = chooser.astype(jnp.float32)
        slot_rows = jnp.transpose(x_rows[:, :, expert_id], (1, 0, 2, 3)).reshape(N_DP, N_EXPERT * CAP, D)
        slot_cots = jnp.transpose(cot_rows[:, :, expert_id], (1, 0, 2, 3)).reshape(N_DP, N_EXPERT * CAP, D)
        packed = jnp.einsum("dls,dsc->dlc", chooser_f, slot_rows.astype(jnp.float32)).astype(jnp.bfloat16)
        packed_cots = jnp.einsum("dls,dsc->dlc", chooser_f, slot_cots.astype(jnp.float32)).astype(jnp.bfloat16)
        packed = packed.reshape(N_DP * LIVE, D)
        packed_cots = packed_cots.reshape(N_DP * LIVE, D)
        keep_mask = jnp.repeat((block_rank[expert_id] < kept_blocks[expert_id]).astype(jnp.float32), BLOCK)
        gate_pre = jnp.dot(packed, w_gate[expert_id], preferred_element_type=jnp.float32)
        up_pre = jnp.dot(packed, w_up[expert_id], preferred_element_type=jnp.float32)
        sigmoid_gate = jax.nn.sigmoid(gate_pre)
        activated = gate_pre * sigmoid_gate
        hidden = (activated * up_pre * keep_mask).astype(jnp.bfloat16)
        hidden_grad = jnp.dot(packed_cots, w_down[expert_id].T, preferred_element_type=jnp.float32)
        up_grad = (hidden_grad * activated * keep_mask).astype(jnp.bfloat16)
        gate_grad = (hidden_grad * up_pre * sigmoid_gate * (1.0 + gate_pre * (1.0 - sigmoid_gate)) * keep_mask).astype(jnp.bfloat16)
        down_parts.append(jnp.dot(hidden.T, packed_cots, preferred_element_type=jnp.float32).astype(jnp.bfloat16))
        gate_parts.append(jnp.dot(packed.T, gate_grad, preferred_element_type=jnp.float32).astype(jnp.bfloat16))
        up_parts.append(jnp.dot(packed.T, up_grad, preferred_element_type=jnp.float32).astype(jnp.bfloat16))
        row_grads = jnp.dot(gate_grad, w_gate[expert_id].T, preferred_element_type=jnp.float32)
        row_grads = row_grads + jnp.dot(up_grad, w_up[expert_id].T, preferred_element_type=jnp.float32)
        row_grads = row_grads.astype(jnp.bfloat16).reshape(N_DP, LIVE, D)
        slot_grads = jnp.einsum("dls,dlc->dsc", chooser_f, row_grads.astype(jnp.float32)).astype(jnp.bfloat16)
        row_parts.append(slot_grads.reshape(N_DP, N_EXPERT, CAP, D))
    grad_rows = jnp.transpose(jnp.stack(row_parts), (2, 1, 0, 3, 4))
    return grad_rows, jnp.stack(gate_parts), jnp.stack(up_parts), jnp.stack(down_parts)
```

```python
import jax
import jax.numpy as jnp
from jax import lax
from jax.sharding import PartitionSpec as P

LIVE = 4


def compact_matrix(slot_counts, live_rows, capacity):
    sources = slot_counts.shape[0]
    within_slot = jnp.tile(jnp.arange(capacity, dtype=jnp.int32), sources)
    count_slot = jnp.repeat(slot_counts, capacity)
    earlier = jnp.arange(sources)[None, :] < jnp.arange(sources)[:, None]
    offsets = jnp.repeat(jnp.sum(jnp.where(earlier, slot_counts[None, :], 0), axis=1), capacity)
    target = offsets + within_slot
    alive = within_slot < count_slot
    row_index = jnp.arange(live_rows, dtype=jnp.int32)[:, None]
    return ((row_index == target[None, :]) & alive[None, :]).astype(jnp.bfloat16)


def contract(left, right, left_dim, right_dim):
    return lax.dot_general(
        left, right, (((left_dim,), (right_dim,)), ((), ())), preferred_element_type=jnp.float32
    )


def body(x_rows, cot_rows, counts, w_gate, w_up, w_down, kept_blocks, block_rank):
    expert_count = x_rows.shape[2]
    capacity = x_rows.shape[3]
    model_width = x_rows.shape[4]
    slot_rows = x_rows.reshape(expert_count, capacity, model_width)
    slot_cots = cot_rows.reshape(expert_count, capacity, model_width)
    my_expert = lax.axis_index("expert")
    picked = jnp.arange(expert_count, dtype=jnp.int32)[None, :] == my_expert
    own_counts = jnp.sum(jnp.where(picked, counts[:, 0, :], 0), axis=1)
    chooser = compact_matrix(own_counts, LIVE, capacity)

    def pack_rows(received):
        flat_rows = received.reshape(-1, model_width)
        return jnp.dot(chooser, flat_rows, preferred_element_type=jnp.float32).astype(jnp.bfloat16)

    got_rows, got_cots = (
        lax.all_to_all(slot_rows, "expert", split_axis=0, concat_axis=0, tiled=True),
        lax.all_to_all(slot_cots, "expert", split_axis=0, concat_axis=0, tiled=True),
    )
    group_rows, group_cots = (
        lax.all_gather(pack_rows(got_rows), "dp", axis=0, tiled=True),
        lax.all_gather(pack_rows(got_cots), "dp", axis=0, tiled=True),
    )
    gate_weight = w_gate[0]
    up_weight = w_up[0]
    down_weight = w_down[0]
    keep_mask = (block_rank.reshape(()) < kept_blocks.reshape(())).astype(jnp.float32)
    gate_pre = jnp.dot(group_rows, gate_weight, preferred_element_type=jnp.float32)
    up_pre = jnp.dot(group_rows, up_weight, preferred_element_type=jnp.float32)
    sigmoid_gate = jax.nn.sigmoid(gate_pre)
    activated = gate_pre * sigmoid_gate
    hidden = (activated * up_pre * keep_mask).astype(jnp.bfloat16)
    hidden_grad = contract(group_cots, down_weight, 1, 1)
    up_grad = (hidden_grad * activated * keep_mask).astype(jnp.bfloat16)
    gate_grad = (
        hidden_grad * up_pre * sigmoid_gate * (1.0 + gate_pre * (1.0 - sigmoid_gate)) * keep_mask
    ).astype(jnp.bfloat16)
    grad_down = contract(hidden, group_cots, 0, 0).astype(jnp.bfloat16)
    grad_gate = contract(group_rows, gate_grad, 0, 0).astype(jnp.bfloat16)
    grad_up = contract(group_rows, up_grad, 0, 0).astype(jnp.bfloat16)
    whole_term = contract(gate_grad, gate_weight, 1, 1) + contract(up_grad, up_weight, 1, 1)
    row_grads = lax.psum_scatter(whole_term, "dp", scatter_dimension=0, tiled=True)
    row_grads = row_grads.astype(jnp.bfloat16)
    slot_grads = contract(chooser, row_grads, 0, 0).astype(jnp.bfloat16)
    slot_grads = slot_grads.reshape(expert_count, capacity, model_width)
    returned = lax.all_to_all(slot_grads, "expert", split_axis=0, concat_axis=0, tiled=True)
    grad_rows = returned.reshape(1, 1, expert_count, capacity, model_width)
    return (grad_rows, grad_gate[None], grad_up[None], grad_down[None])


def solution(mesh):
    in_specs = (
        P("expert", "dp", None, None, None),
        P("expert", "dp", None, None, None),
        P(None, "dp", None),
        P("expert", None, "dp"),
        P("expert", None, "dp"),
        P("expert", "dp", None),
        P("expert"),
        P("expert", "dp"),
    )
    out_specs = (
        P("expert", "dp", None, None, None),
        P("expert", None, "dp"),
        P("expert", None, "dp"),
        P("expert", "dp", None),
    )
    return jax.shard_map(body, mesh=mesh, in_specs=in_specs, out_specs=out_specs, check_vma=False)
```

```python
import jax
import jax.numpy as jnp
import numpy as np
from jax import lax
from jax.sharding import Mesh
from jax.sharding import PartitionSpec as P

LIVE = 4
EXPERT = ("z_lo", "core")
PLANE = ("x", "y")
DP = ("z_hi", "x", "y")


def contract(left, right, left_dim, right_dim):
    return lax.dot_general(
        left, right, (((left_dim,), (right_dim,)), ((), ())), preferred_element_type=jnp.float32
    )


def compact_matrix(slot_counts, capacity):
    sources = slot_counts.shape[0]
    earlier = jnp.arange(sources)[None, :] < jnp.arange(sources)[:, None]
    offsets = jnp.sum(jnp.where(earlier, slot_counts[None, :], 0), axis=1)
    within = jnp.arange(capacity, dtype=jnp.int32)[None, :]
    target = jnp.where(within < slot_counts[:, None], offsets[:, None] + within, -1)
    row = jnp.arange(LIVE, dtype=jnp.int32)[:, None, None]
    return (row == target[None]).astype(jnp.bfloat16)


def exchange(array, axes):
    return lax.all_to_all(array, axes, split_axis=0, concat_axis=0, tiled=True)


def spread(array, axes, size):
    return exchange(jnp.broadcast_to(array[None], (size,) + array.shape), axes)


def body(x_rows, cot_rows, counts, w_gate, w_up, w_down, kept_blocks, block_rank):
    experts, capacity, width = x_rows.shape[2:]
    my_expert = lax.axis_index(EXPERT)
    picked = jnp.arange(experts, dtype=jnp.int32)[None, :] == my_expert
    own_counts = jnp.sum(jnp.where(picked, counts[:, 0, :], 0), axis=1)
    chooser = compact_matrix(own_counts, capacity)
    none = jnp.zeros_like(chooser)
    both = jnp.concatenate(
        (jnp.concatenate((chooser, none), 2), jnp.concatenate((none, chooser), 2)), 0
    ).reshape(2 * LIVE, 2 * experts * capacity)

    slots = jnp.concatenate((x_rows[0, 0], cot_rows[0, 0]), axis=1)
    got = exchange(slots, EXPERT).reshape(2 * experts * capacity, width)
    packed = jnp.dot(both, got, preferred_element_type=jnp.float32).astype(jnp.bfloat16)
    column = spread(packed, "z_hi", 4)
    column = column.reshape(4, 2, LIVE, width).transpose(1, 0, 2, 3).reshape(8 * LIVE, width)
    group = spread(column, PLANE, 16)
    rows = group[:, : 4 * LIVE].reshape(64 * LIVE, width)
    cots = group[:, 4 * LIVE :].reshape(64 * LIVE, width)

    gate_weight, up_weight, down_weight = w_gate[0], w_up[0], w_down[0]
    keep = (block_rank.reshape(()) < kept_blocks.reshape(())).astype(jnp.float32)
    gate = jnp.dot(rows, gate_weight, preferred_element_type=jnp.float32)
    up = jnp.dot(rows, up_weight, preferred_element_type=jnp.float32)
    hidden_grad = contract(cots, down_weight, 1, 1)
    sig = jax.nn.sigmoid(gate)
    act = gate * sig
    hidden = (act * up * keep).astype(jnp.bfloat16)
    up_grad = (hidden_grad * act * keep).astype(jnp.bfloat16)
    gate_grad = (hidden_grad * up * sig * (1.0 + gate * (1.0 - sig)) * keep).astype(jnp.bfloat16)
    term = contract(gate_grad, gate_weight, 1, 1) + contract(up_grad, up_weight, 1, 1)
    parts = exchange(term.astype(jnp.bfloat16).reshape(16, 4 * LIVE, width), PLANE)
    plane_sum = jnp.sum(parts.astype(jnp.float32), axis=0).astype(jnp.bfloat16)
    parts = exchange(plane_sum.reshape(4, LIVE, width), "z_hi")
    row_grads = jnp.sum(parts.astype(jnp.float32), axis=0).astype(jnp.bfloat16)
    slot_grads = contract(chooser.reshape(LIVE, experts * capacity), row_grads, 0, 0)
    slot_grads = slot_grads.astype(jnp.bfloat16).reshape(experts, capacity, width)
    grad_rows = exchange(slot_grads, EXPERT)[None, None]

    grad_down = contract(hidden, cots, 0, 0).astype(jnp.bfloat16)
    grad_gate = contract(rows, gate_grad, 0, 0).astype(jnp.bfloat16)
    grad_up = contract(rows, up_grad, 0, 0).astype(jnp.bfloat16)
    return (grad_rows, grad_gate[None], grad_up[None], grad_down[None])


def solution(mesh):
    fine = Mesh(np.asarray(mesh.devices).reshape(4, 2, 4, 4, 4), EXPERT + DP)
    in_specs = (
        P(EXPERT, DP, None, None, None),
        P(EXPERT, DP, None, None, None),
        P(None, DP, None),
        P(EXPERT, None, DP),
        P(EXPERT, None, DP),
        P(EXPERT, DP, None),
        P(EXPERT),
        P(EXPERT, DP),
    )
    out_specs = (
        P(EXPERT, DP, None, None, None),
        P(EXPERT, None, DP),
        P(EXPERT, None, DP),
        P(EXPERT, DP, None),
    )
    return jax.shard_map(body, mesh=fine, in_specs=in_specs, out_specs=out_specs, check_vma=False)
```

```python
import jax
import jax.numpy as jnp
import numpy as np
from jax import lax
from jax.experimental import pallas as pl
from jax.experimental.pallas import tpu as pltpu
from jax.sharding import Mesh
from jax.sharding import PartitionSpec as P

LIVE = 4
EXPERT = ("z_lo", "core")
PLANE = ("x", "y")
DP = ("z_hi", "x", "y")
STEP = 512
NN = (((1,), (0,)), ((), ()))
NT = (((1,), (1,)), ((), ()))
TN = (((0,), (0,)), ((), ()))
VMEM_LIMIT = 40 * 2**20


def dot(left, right, dims=NN):
    return lax.dot_general(left, right, dims, preferred_element_type=jnp.float32)


def compact_matrix(slot_counts, capacity):
    sources = slot_counts.shape[0]
    earlier = jnp.arange(sources)[None, :] < jnp.arange(sources)[:, None]
    offsets = jnp.sum(jnp.where(earlier, slot_counts[None, :], 0), axis=1)
    within = jnp.arange(capacity, dtype=jnp.int32)[None, :]
    target = jnp.where(within < slot_counts[:, None], offsets[:, None] + within, -1)
    row = jnp.arange(LIVE, dtype=jnp.int32)[:, None, None]
    return (row == target[None]).astype(jnp.bfloat16)


def exchange(array, axes):
    return lax.all_to_all(array, axes, split_axis=0, concat_axis=0, tiled=True)


def fan_kernel(column, fan, ordered, sems):
    size = column.shape[0]
    out = lax.broadcasted_iota(jnp.int32, (size, size), 0)
    source = ((out & 15) >> 2) * 8 + (out >> 4) * 4 + (out & 3)
    order = (source == lax.broadcasted_iota(jnp.int32, (size, size), 1)).astype(jnp.bfloat16)
    ordered[...] = dot(order, column[...]).astype(jnp.bfloat16)
    copies = [
        pltpu.make_async_copy(ordered, fan.at[i], sems.at[i]) for i in range(fan.shape[0])
    ]
    for copy in copies:
        copy.start()
    for copy in copies:
        copy.wait()


def fan_out(column, receivers):
    size, width = column.shape
    return pl.pallas_call(
        fan_kernel,
        out_shape=jax.ShapeDtypeStruct((receivers, size, width), jnp.bfloat16),
        in_specs=[pl.BlockSpec(memory_space=pltpu.VMEM)],
        out_specs=pl.BlockSpec(memory_space=pl.ANY),
        scratch_shapes=[
            pltpu.VMEM((size, width), jnp.bfloat16),
            pltpu.SemaphoreType.DMA((receivers,)),
        ],
        compiler_params=pltpu.CompilerParams(vmem_limit_bytes=VMEM_LIMIT),
    )(column)


def middle_kernel(
    keep_row, group, w_gate, w_up, w_down, term, hidden, gate_grad, up_grad, sums, both
):
    blocks, pair, width = group.shape
    half = pair // 2
    size = blocks * half
    sums[...] = jnp.zeros_like(sums)

    def forward(i, carry):
        part = pl.ds(pl.multiple_of(i * STEP, STEP), STEP)
        rows = group[:, :half, part].reshape(size, STEP)
        cots = group[:, half:, part].reshape(size, STEP)
        sums[0] += dot(rows, w_gate[part, :])
        sums[1] += dot(rows, w_up[part, :])
        sums[2] += dot(cots, w_down[:, part], NT)
        return carry

    lax.fori_loop(0, width // STEP, forward, 0)
    keep = keep_row[0:1, :]
    gate, up, hidden_grad = sums[0], sums[1], sums[2]
    sig = jax.nn.sigmoid(gate)
    act = gate * sig
    hidden[...] = (act * up * keep).astype(jnp.bfloat16)
    dup = (hidden_grad * act * keep).astype(jnp.bfloat16)
    dgate = (hidden_grad * up * sig * (1.0 + gate * (1.0 - sig)) * keep).astype(jnp.bfloat16)
    up_grad[...] = dup
    gate_grad[...] = dgate
    both[...] = jnp.concatenate((dgate, dup), axis=1)

    def backward(i, carry):
        part = pl.ds(pl.multiple_of(i * STEP, STEP), STEP)
        weights = jnp.concatenate((w_gate[part, :], w_up[part, :]), axis=1)
        out = dot(both[...], weights, NT).astype(jnp.bfloat16)
        term[:, :, part] = out.reshape(blocks, half, STEP)
        return carry

    lax.fori_loop(0, width // STEP, backward, 0)


def middle(keep, group, w_gate, w_up, w_down):
    blocks, pair, width = group.shape
    units = w_gate.shape[1]
    size = blocks * pair // 2
    vmem = pl.BlockSpec(memory_space=pltpu.VMEM)
    grads = jax.ShapeDtypeStruct((size, units), jnp.bfloat16)
    return pl.pallas_call(
        middle_kernel,
        out_shape=(
            jax.ShapeDtypeStruct((blocks, pair // 2, width), jnp.bfloat16),
            grads,
            grads,
            grads,
        ),
        in_specs=[vmem, vmem, vmem, vmem, vmem],
        out_specs=(vmem, vmem, vmem, vmem),
        scratch_shapes=[
            pltpu.VMEM((3, size, units), jnp.float32),
            pltpu.VMEM((size, 2 * units), jnp.bfloat16),
        ],
        compiler_params=pltpu.CompilerParams(vmem_limit_bytes=VMEM_LIMIT),
        cost_estimate=pl.CostEstimate(
            flops=10 * size * units * width, bytes_accessed=8 * 2**20, transcendentals=size * units
        ),
    )(keep, group, w_gate, w_up, w_down)


def body(x_rows, cot_rows, counts, w_gate, w_up, w_down, kept_blocks, block_rank):
    experts, capacity, width = x_rows.shape[2:]
    my_expert = lax.axis_index(EXPERT)
    picked = jnp.arange(experts, dtype=jnp.int32)[None, :] == my_expert
    own_counts = jnp.sum(jnp.where(picked, counts[:, 0, :], 0), axis=1)
    chooser = compact_matrix(own_counts, capacity)
    back = chooser.reshape(LIVE, experts * capacity).T
    kind = jnp.eye(2, dtype=jnp.bfloat16)
    both = kind[:, None, None, :, None] * chooser[None, :, :, None, :]
    both = both.reshape(2 * LIVE, experts * 2 * capacity)

    slots = jnp.stack((x_rows[0, 0], cot_rows[0, 0]), axis=1)
    keep = (block_rank.reshape(()) < kept_blocks.reshape(())).astype(jnp.float32)
    keep = jnp.broadcast_to(keep, (8, w_gate.shape[2]))
    got = exchange(slots, EXPERT)
    got, both, back, keep = lax.optimization_barrier((got, both, back, keep))
    got = got.reshape(experts * 2 * capacity, width)
    packed = dot(both, got).astype(jnp.bfloat16)
    column = lax.all_gather(packed, "z_hi", axis=0, tiled=True)
    group = exchange(fan_out(column, 16), PLANE)
    term, hidden, gate_grad, up_grad = middle(
        keep, group, w_gate[0], w_up[0], w_down[0]
    )
    parts = exchange(term, PLANE)
    plane_sum = jnp.sum(parts.astype(jnp.float32), axis=0).astype(jnp.bfloat16)
    plane_sum, hidden, gate_grad, up_grad = lax.optimization_barrier(
        (plane_sum, hidden, gate_grad, up_grad)
    )
    parts = exchange(plane_sum.reshape(4, LIVE, width), "z_hi")
    row_grads = jnp.sum(parts.astype(jnp.float32), axis=0).astype(jnp.bfloat16)
    slot_grads = dot(back, row_grads)
    slot_grads = slot_grads.astype(jnp.bfloat16).reshape(experts, capacity, width)
    grad_rows = exchange(slot_grads, EXPERT)[None, None]

    rows = group[:, : 4 * LIVE].reshape(64 * LIVE, width)
    cots = group[:, 4 * LIVE :].reshape(64 * LIVE, width)
    grad_down = dot(hidden, cots, TN).astype(jnp.bfloat16)
    grad_gate = dot(rows, gate_grad, TN).astype(jnp.bfloat16)
    grad_up = dot(rows, up_grad, TN).astype(jnp.bfloat16)
    return (grad_rows, grad_gate[None], grad_up[None], grad_down[None])


def solution(mesh):
    fine = Mesh(np.asarray(mesh.devices).reshape(4, 2, 4, 4, 4), EXPERT + DP)
    in_specs = (
        P(EXPERT, DP, None, None, None),
        P(EXPERT, DP, None, None, None),
        P(None, DP, None),
        P(EXPERT, None, DP),
        P(EXPERT, None, DP),
        P(EXPERT, DP, None),
        P(EXPERT),
        P(EXPERT, DP),
    )
    out_specs = (
        P(EXPERT, DP, None, None, None),
        P(EXPERT, None, DP),
        P(EXPERT, None, DP),
        P(EXPERT, DP, None),
    )
    return jax.shard_map(body, mesh=fine, in_specs=in_specs, out_specs=out_specs, check_vma=False)
```

```python
import jax
import jax.numpy as jnp
import numpy as np
from jax import lax
from jax.experimental import pallas as pl
from jax.experimental.pallas import tpu as pltpu
from jax.sharding import Mesh
from jax.sharding import PartitionSpec as P

LIVE = 4
EXPERT = ("z_lo", "core")
DP = ("z_hi", "x", "y")
STEP = 512
NN = (((1,), (0,)), ((), ()))
NT = (((1,), (1,)), ((), ()))
TN = (((0,), (0,)), ((), ()))
VMEM_LIMIT = 40 * 2**20


def dot(left, right, dims=NN):
    return lax.dot_general(left, right, dims, preferred_element_type=jnp.float32)


def compact_matrix(slot_counts, capacity):
    sources = slot_counts.shape[0]
    earlier = jnp.arange(sources)[None, :] < jnp.arange(sources)[:, None]
    offsets = jnp.sum(jnp.where(earlier, slot_counts[None, :], 0), axis=1)
    within = jnp.arange(capacity, dtype=jnp.int32)[None, :]
    target = jnp.where(within < slot_counts[:, None], offsets[:, None] + within, -1)
    row = jnp.arange(LIVE, dtype=jnp.int32)[:, None, None]
    return (row == target[None]).astype(jnp.bfloat16)


CHIP_PLANE = ("core", "x", "y")
ALONG_X = [[x * 4 + y for x in range(4)] for y in range(4)]
ALONG_Y = [[x * 4 + y for y in range(4)] for x in range(4)]


def per_core(first, second):
    return first + [[16 + place for place in group] for group in second]


NEAR = per_core(ALONG_X, ALONG_Y)
FAR = per_core(ALONG_Y, ALONG_X)
WHOLE = per_core([sum(ALONG_X, [])], [sum(ALONG_Y, [])])


def exchange(array, axes, groups=None):
    return lax.all_to_all(
        array, axes, split_axis=0, concat_axis=0, axis_index_groups=groups, tiled=True
    )


def order_kernel(column, fan):
    size = column.shape[0]
    out = lax.broadcasted_iota(jnp.int32, (size, size), 0)
    source = ((out & 15) >> 2) * 8 + (out >> 4) * 4 + (out & 3)
    order = (source == lax.broadcasted_iota(jnp.int32, (size, size), 1)).astype(jnp.bfloat16)
    ordered = dot(order, column[...]).astype(jnp.bfloat16)
    for i in range(fan.shape[0]):
        fan[i] = ordered


def copy_kernel(block, fan):
    for i in range(fan.shape[0]):
        fan[i] = block[...]


def fan_out(kernel, block, receivers):
    return pl.pallas_call(
        kernel,
        out_shape=jax.ShapeDtypeStruct((receivers,) + block.shape, jnp.bfloat16),
        in_specs=[pl.BlockSpec(memory_space=pltpu.VMEM)],
        out_specs=pl.BlockSpec(memory_space=pltpu.VMEM),
        compiler_params=pltpu.CompilerParams(vmem_limit_bytes=VMEM_LIMIT),
    )(block)


def middle_kernel(
    keep_row, group, w_gate, w_up, w_down, term, hidden, gate_grad, up_grad, sums, both
):
    blocks, pair, width = group.shape
    half = pair // 2
    size = blocks * half
    sums[...] = jnp.zeros_like(sums)

    def forward(i, carry):
        part = pl.ds(pl.multiple_of(i * STEP, STEP), STEP)
        rows = group[:, :half, part].reshape(size, STEP)
        cots = group[:, half:, part].reshape(size, STEP)
        sums[0] += dot(rows, w_gate[part, :])
        sums[1] += dot(rows, w_up[part, :])
        sums[2] += dot(cots, w_down[:, part], NT)
        return carry

    lax.fori_loop(0, width // STEP, forward, 0)
    keep = keep_row[0:1, :]
    gate, up, hidden_grad = sums[0], sums[1], sums[2]
    sig = jax.nn.sigmoid(gate)
    act = gate * sig
    hidden[...] = (act * up * keep).astype(jnp.bfloat16)
    dup = (hidden_grad * act * keep).astype(jnp.bfloat16)
    dgate = (hidden_grad * up * sig * (1.0 + gate * (1.0 - sig)) * keep).astype(jnp.bfloat16)
    up_grad[...] = dup
    gate_grad[...] = dgate
    both[...] = jnp.concatenate((dgate, dup), axis=1)

    def backward(i, carry):
        part = pl.ds(pl.multiple_of(i * STEP, STEP), STEP)
        weights = jnp.concatenate((w_gate[part, :], w_up[part, :]), axis=1)
        out = dot(both[...], weights, NT).astype(jnp.bfloat16)
        term[:, :, part] = out.reshape(blocks, half, STEP)
        return carry

    lax.fori_loop(0, width // STEP, backward, 0)


def middle(keep, group, w_gate, w_up, w_down):
    blocks, pair, width = group.shape
    units = w_gate.shape[1]
    size = blocks * pair // 2
    vmem = pl.BlockSpec(memory_space=pltpu.VMEM)
    grads = jax.ShapeDtypeStruct((size, units), jnp.bfloat16)
    return pl.pallas_call(
        middle_kernel,
        out_shape=(
            jax.ShapeDtypeStruct((blocks, pair // 2, width), jnp.bfloat16),
            grads,
            grads,
            grads,
        ),
        in_specs=[vmem, vmem, vmem, vmem, vmem],
        out_specs=(vmem, vmem, vmem, vmem),
        scratch_shapes=[
            pltpu.VMEM((3, size, units), jnp.float32),
            pltpu.VMEM((size, 2 * units), jnp.bfloat16),
        ],
        compiler_params=pltpu.CompilerParams(vmem_limit_bytes=VMEM_LIMIT),
        cost_estimate=pl.CostEstimate(
            flops=10 * size * units * width, bytes_accessed=8 * 2**20, transcendentals=size * units
        ),
    )(keep, group, w_gate, w_up, w_down)


def body(x_rows, cot_rows, counts, w_gate, w_up, w_down, kept_blocks, block_rank):
    experts, capacity, width = x_rows.shape[2:]
    my_expert = lax.axis_index(EXPERT)
    picked = jnp.arange(experts, dtype=jnp.int32)[None, :] == my_expert
    own_counts = jnp.sum(jnp.where(picked, counts[:, 0, :], 0), axis=1)
    chooser = compact_matrix(own_counts, capacity)
    back = chooser.reshape(LIVE, experts * capacity).T
    kind = jnp.eye(2, dtype=jnp.bfloat16)
    both = kind[:, None, None, :, None] * chooser[None, :, :, None, :]
    both = both.reshape(2 * LIVE, experts * 2 * capacity)

    slots = jnp.stack((x_rows[0, 0], cot_rows[0, 0]), axis=1)
    keep = (block_rank.reshape(()) < kept_blocks.reshape(())).astype(jnp.float32)
    keep = jnp.broadcast_to(keep, (8, w_gate.shape[2]))
    got = exchange(slots, EXPERT)
    got, both, back, keep = lax.optimization_barrier((got, both, back, keep))
    got = got.reshape(experts * 2 * capacity, width)
    packed = dot(both, got).astype(jnp.bfloat16)
    column = lax.all_gather(packed, "z_hi", axis=0, tiled=True)
    line = exchange(fan_out(order_kernel, column, 4), CHIP_PLANE, NEAR)
    group = exchange(fan_out(copy_kernel, line, 4), CHIP_PLANE, FAR)
    group = group.reshape(16, 8 * LIVE, width)
    term, hidden, gate_grad, up_grad = middle(
        keep, group, w_gate[0], w_up[0], w_down[0]
    )
    parts = exchange(term, CHIP_PLANE, WHOLE)
    plane_sum = jnp.sum(parts.astype(jnp.float32), axis=0).astype(jnp.bfloat16)
    plane_sum, group, hidden, gate_grad, up_grad = lax.optimization_barrier(
        (plane_sum, group, hidden, gate_grad, up_grad)
    )
    parts = exchange(plane_sum.reshape(4, LIVE, width), "z_hi")
    rows = group[:, : 4 * LIVE].reshape(64 * LIVE, width)
    cots = group[:, 4 * LIVE :].reshape(64 * LIVE, width)
    grad_down = dot(hidden, cots, TN).astype(jnp.bfloat16)
    grad_gate = dot(rows, gate_grad, TN).astype(jnp.bfloat16)
    grad_up = dot(rows, up_grad, TN).astype(jnp.bfloat16)
    parts, grad_gate, grad_up, grad_down = lax.optimization_barrier(
        (parts, grad_gate, grad_up, grad_down)
    )
    row_grads = jnp.sum(parts.astype(jnp.float32), axis=0).astype(jnp.bfloat16)
    slot_grads = dot(back, row_grads)
    slot_grads = slot_grads.astype(jnp.bfloat16).reshape(experts, capacity, width)
    grad_rows = exchange(slot_grads, EXPERT)[None, None]
    return (grad_rows, grad_gate[None], grad_up[None], grad_down[None])


def solution(mesh):
    fine = Mesh(np.asarray(mesh.devices).reshape(4, 2, 4, 4, 4), EXPERT + DP)
    in_specs = (
        P(EXPERT, DP, None, None, None),
        P(EXPERT, DP, None, None, None),
        P(None, DP, None),
        P(EXPERT, None, DP),
        P(EXPERT, None, DP),
        P(EXPERT, DP, None),
        P(EXPERT),
        P(EXPERT, DP),
    )
    out_specs = (
        P(EXPERT, DP, None, None, None),
        P(EXPERT, None, DP),
        P(EXPERT, None, DP),
        P(EXPERT, DP, None),
    )
    return jax.shard_map(body, mesh=fine, in_specs=in_specs, out_specs=out_specs, check_vma=False)
```

```python
import jax
import jax.numpy as jnp
import numpy as np
from jax import lax
from jax.experimental import pallas as pl
from jax.experimental.pallas import tpu as pltpu
from jax.sharding import Mesh
from jax.sharding import PartitionSpec as P

LIVE = 4
EXPERT = ("z_lo", "core")
DP = ("z_hi", "x", "y")
STEP = 512
NN = (((1,), (0,)), ((), ()))
NT = (((1,), (1,)), ((), ()))
TN = (((0,), (0,)), ((), ()))
VMEM_LIMIT = 40 * 2**20


def dot(left, right, dims=NN):
    return lax.dot_general(left, right, dims, preferred_element_type=jnp.float32)


def compact_matrix(slot_counts, capacity):
    sources = slot_counts.shape[0]
    earlier = jnp.arange(sources)[None, :] < jnp.arange(sources)[:, None]
    offsets = jnp.sum(jnp.where(earlier, slot_counts[None, :], 0), axis=1)
    within = jnp.arange(capacity, dtype=jnp.int32)[None, :]
    target = jnp.where(within < slot_counts[:, None], offsets[:, None] + within, -1)
    row = jnp.arange(LIVE, dtype=jnp.int32)[:, None, None]
    return (row == target[None]).astype(jnp.bfloat16)


CHIP_PLANE = ("core", "x", "y")
ALONG_X = [[x * 4 + y for x in range(4)] for y in range(4)]
ALONG_Y = [[x * 4 + y for y in range(4)] for x in range(4)]


def per_core(first, second):
    return first + [[16 + place for place in group] for group in second]


NEAR = per_core(ALONG_X, ALONG_Y)
WHOLE = per_core([sum(ALONG_X, [])], [sum(ALONG_Y, [])])


def far_step(by):
    along_y = [(x * 4 + y, x * 4 + (y + by) % 4) for x in range(4) for y in range(4)]
    along_x = [(16 + x * 4 + y, 16 + (x + by) % 4 * 4 + y) for x in range(4) for y in range(4)]
    return along_y + along_x


def send(array, by):
    return lax.ppermute(array, CHIP_PLANE, far_step(by))


def exchange(array, axes, groups=None):
    return lax.all_to_all(
        array, axes, split_axis=0, concat_axis=0, axis_index_groups=groups, tiled=True
    )


def order_kernel(column, fan):
    size = column.shape[0]
    out = lax.broadcasted_iota(jnp.int32, (size, size), 0)
    source = ((out & 15) >> 2) * 8 + (out >> 4) * 4 + (out & 3)
    order = (source == lax.broadcasted_iota(jnp.int32, (size, size), 1)).astype(jnp.bfloat16)
    ordered = dot(order, column[...]).astype(jnp.bfloat16)
    for i in range(fan.shape[0]):
        fan[i] = ordered


def fan_out(kernel, block, receivers):
    return pl.pallas_call(
        kernel,
        out_shape=jax.ShapeDtypeStruct((receivers,) + block.shape, jnp.bfloat16),
        in_specs=[pl.BlockSpec(memory_space=pltpu.VMEM)],
        out_specs=pl.BlockSpec(memory_space=pltpu.VMEM),
        compiler_params=pltpu.CompilerParams(vmem_limit_bytes=VMEM_LIMIT),
    )(block)


def middle_kernel(keep_row, *refs):
    group, (w_gate, w_up, w_down) = refs[:7], refs[7:10]
    term, rows, cots, hidden, gate_grad, up_grad, sums, both = refs[10:]
    blocks, half, width = term.shape
    size = blocks * half
    core = lax.axis_index("core")
    place = jnp.where(core == 0, lax.axis_index("y"), lax.axis_index("x"))
    sums[...] = jnp.zeros_like(sums)

    def forward(i, carry):
        part = pl.ds(pl.multiple_of(i * STEP, STEP), STEP)
        start = 0
        for block in group:
            count = block.shape[0] * half
            rows[start : start + count, part] = block[:, :half, part].reshape(count, STEP)
            cots[start : start + count, part] = block[:, half:, part].reshape(count, STEP)
            start += count
        sums[0] += dot(rows[:, part], w_gate[part, :])
        sums[1] += dot(rows[:, part], w_up[part, :])
        sums[2] += dot(cots[:, part], w_down[:, part], NT)
        return carry

    lax.fori_loop(0, width // STEP, forward, 0)
    keep = keep_row[0:1, :]
    gate, up, hidden_grad = sums[0], sums[1], sums[2]
    sig = jax.nn.sigmoid(gate)
    act = gate * sig
    hidden[...] = (act * up * keep).astype(jnp.bfloat16)
    dup = (hidden_grad * act * keep).astype(jnp.bfloat16)
    dgate = (hidden_grad * up * sig * (1.0 + gate * (1.0 - sig)) * keep).astype(jnp.bfloat16)
    up_grad[...] = dup
    gate_grad[...] = dgate
    both[...] = jnp.concatenate((dgate, dup), axis=1)

    def backward(i, carry):
        part = pl.ds(pl.multiple_of(i * STEP, STEP), STEP)
        weights = jnp.concatenate((w_gate[part, :], w_up[part, :]), axis=1)
        out = dot(both[...], weights, NT).astype(jnp.bfloat16)
        for j, by in enumerate((0, 3, 1, 2)):
            line = out[j * size // 4 : (j + 1) * size // 4].reshape(blocks // 4, half, STEP)
            term[pl.ds(((place + by) & 3) * (blocks // 4), blocks // 4), :, part] = line
        return carry

    lax.fori_loop(0, width // STEP, backward, 0)


def middle(keep, group, w_gate, w_up, w_down):
    blocks = sum(block.shape[0] for block in group)
    pair, width = group[0].shape[1:]
    units = w_gate.shape[1]
    size = blocks * pair // 2
    vmem = pl.BlockSpec(memory_space=pltpu.VMEM)
    rows = jax.ShapeDtypeStruct((size, width), jnp.bfloat16)
    grads = jax.ShapeDtypeStruct((size, units), jnp.bfloat16)
    return pl.pallas_call(
        middle_kernel,
        out_shape=(
            jax.ShapeDtypeStruct((blocks, pair // 2, width), jnp.bfloat16),
            rows,
            rows,
            grads,
            grads,
            grads,
        ),
        in_specs=[vmem] * 11,
        out_specs=(vmem,) * 6,
        scratch_shapes=[
            pltpu.VMEM((3, size, units), jnp.float32),
            pltpu.VMEM((size, 2 * units), jnp.bfloat16),
        ],
        compiler_params=pltpu.CompilerParams(vmem_limit_bytes=VMEM_LIMIT),
        cost_estimate=pl.CostEstimate(
            flops=10 * size * units * width, bytes_accessed=8 * 2**20, transcendentals=size * units
        ),
    )(keep, *group, w_gate, w_up, w_down)


def body(x_rows, cot_rows, counts, w_gate, w_up, w_down, kept_blocks, block_rank):
    experts, capacity, width = x_rows.shape[2:]
    my_expert = lax.axis_index(EXPERT)
    picked = jnp.arange(experts, dtype=jnp.int32)[None, :] == my_expert
    own_counts = jnp.sum(jnp.where(picked, counts[:, 0, :], 0), axis=1)
    chooser = compact_matrix(own_counts, capacity)
    back = chooser.reshape(LIVE, experts * capacity).T
    kind = jnp.eye(2, dtype=jnp.bfloat16)
    both = kind[:, None, None, :, None] * chooser[None, :, :, None, :]
    both = both.reshape(2 * LIVE, experts * 2 * capacity)

    slots = jnp.stack((x_rows[0, 0], cot_rows[0, 0]), axis=1)
    keep = (block_rank.reshape(()) < kept_blocks.reshape(())).astype(jnp.float32)
    keep = jnp.broadcast_to(keep, (8, w_gate.shape[2]))
    got = exchange(slots, EXPERT)
    got, both, back, keep = lax.optimization_barrier((got, both, back, keep))
    got = got.reshape(experts * 2 * capacity, width)
    packed = dot(both, got).astype(jnp.bfloat16)
    column = lax.all_gather(packed, "z_hi", axis=0, tiled=True)
    line = exchange(fan_out(order_kernel, column, 4), CHIP_PLANE, NEAR)
    low, high = line[:2], line[2:]
    left_low, right_high = send(low, 1), send(high, -1)
    left_high, right_low = send(high, 1), send(low, -1)
    far_low, far_high = send(left_low, 1), send(right_high, -1)
    group = (line, left_low, left_high, right_low, right_high, far_low, far_high)
    term, rows, cots, hidden, gate_grad, up_grad = middle(keep, group, w_gate[0], w_up[0], w_down[0])
    parts = exchange(term, CHIP_PLANE, WHOLE)
    plane_sum = jnp.sum(parts.astype(jnp.float32), axis=0).astype(jnp.bfloat16)
    plane_sum, rows, cots, hidden, gate_grad, up_grad = lax.optimization_barrier(
        (plane_sum, rows, cots, hidden, gate_grad, up_grad)
    )
    parts = exchange(plane_sum.reshape(4, LIVE, width), "z_hi")
    grad_down = dot(hidden, cots, TN).astype(jnp.bfloat16)
    grad_gate = dot(rows, gate_grad, TN).astype(jnp.bfloat16)
    grad_up = dot(rows, up_grad, TN).astype(jnp.bfloat16)
    parts, grad_gate, grad_up, grad_down = lax.optimization_barrier(
        (parts, grad_gate, grad_up, grad_down)
    )
    row_grads = jnp.sum(parts.astype(jnp.float32), axis=0).astype(jnp.bfloat16)
    slot_grads = dot(back, row_grads)
    slot_grads = slot_grads.astype(jnp.bfloat16).reshape(experts, capacity, width)
    grad_rows = exchange(slot_grads, EXPERT)[None, None]
    return (grad_rows, grad_gate[None], grad_up[None], grad_down[None])


def solution(mesh):
    fine = Mesh(np.asarray(mesh.devices).reshape(4, 2, 4, 4, 4), EXPERT + DP)
    in_specs = (
        P(EXPERT, DP, None, None, None),
        P(EXPERT, DP, None, None, None),
        P(None, DP, None),
        P(EXPERT, None, DP),
        P(EXPERT, None, DP),
        P(EXPERT, DP, None),
        P(EXPERT),
        P(EXPERT, DP),
    )
    out_specs = (
        P(EXPERT, DP, None, None, None),
        P(EXPERT, None, DP),
        P(EXPERT, None, DP),
        P(EXPERT, DP, None),
    )
    return jax.shard_map(body, mesh=fine, in_specs=in_specs, out_specs=out_specs, check_vma=False)
```

```python
import jax
import jax.numpy as jnp
import numpy as np
from jax import lax
from jax.experimental import pallas as pl
from jax.experimental.pallas import tpu as pltpu
from jax.sharding import Mesh
from jax.sharding import PartitionSpec as P

LIVE = 4
EXPERT = ("z_lo", "core")
DP = ("z_hi", "x", "y")
STEP = 512
NN = (((1,), (0,)), ((), ()))
NT = (((1,), (1,)), ((), ()))
TN = (((0,), (0,)), ((), ()))
VMEM_LIMIT = 40 * 2**20


def dot(left, right, dims=NN):
    return lax.dot_general(left, right, dims, preferred_element_type=jnp.float32)


def compact_matrix(slot_counts, capacity):
    sources = slot_counts.shape[0]
    earlier = jnp.arange(sources)[None, :] < jnp.arange(sources)[:, None]
    offsets = jnp.sum(jnp.where(earlier, slot_counts[None, :], 0), axis=1)
    within = jnp.arange(capacity, dtype=jnp.int32)[None, :]
    target = jnp.where(within < slot_counts[:, None], offsets[:, None] + within, -1)
    row = jnp.arange(LIVE, dtype=jnp.int32)[:, None, None]
    return (row == target[None]).astype(jnp.bfloat16)


CHIP_PLANE = ("core", "x", "y")
ALONG_X = [[x * 4 + y for x in range(4)] for y in range(4)]
ALONG_Y = [[x * 4 + y for y in range(4)] for x in range(4)]


def per_core(first, second):
    return first + [[16 + place for place in group] for group in second]


WHOLE = per_core([sum(ALONG_X, [])], [sum(ALONG_Y, [])])


def exchange(array, axes, groups=None):
    return lax.all_to_all(
        array, axes, split_axis=0, concat_axis=0, axis_index_groups=groups, tiled=True
    )


def order_kernel(column, fan):
    size = column.shape[0]
    out = lax.broadcasted_iota(jnp.int32, (size, size), 0)
    source = ((out & 15) >> 2) * 8 + (out >> 4) * 4 + (out & 3)
    order = (source == lax.broadcasted_iota(jnp.int32, (size, size), 1)).astype(jnp.bfloat16)
    ordered = dot(order, column[...]).astype(jnp.bfloat16)
    for i in range(fan.shape[0]):
        fan[i] = ordered


def fan_out(block, receivers):
    return pl.pallas_call(
        order_kernel,
        out_shape=jax.ShapeDtypeStruct((receivers,) + block.shape, jnp.bfloat16),
        in_specs=[pl.BlockSpec(memory_space=pltpu.VMEM)],
        out_specs=pl.BlockSpec(memory_space=pltpu.VMEM),
        compiler_params=pltpu.CompilerParams(vmem_limit_bytes=VMEM_LIMIT),
    )(block)


def middle_kernel(
    keep_row, group, w_gate, w_up, w_down, term, hidden, gate_grad, up_grad, sums, both
):
    blocks, pair, width = group.shape
    half = pair // 2
    size = blocks * half
    units = w_gate.shape[1]
    sums[...] = jnp.zeros_like(sums)

    def forward(i, carry):
        part = pl.ds(pl.multiple_of(i * STEP, STEP), STEP)
        rows = group[:, :half, part].reshape(size, STEP)
        cots = group[:, half:, part].reshape(size, STEP)
        weights = jnp.concatenate((w_gate[part, :], w_up[part, :]), axis=1)
        sums[:, : 2 * units] += dot(rows, weights)
        sums[:, 2 * units :] += dot(cots, w_down[:, part], NT)
        return carry

    lax.fori_loop(0, width // STEP, forward, 0)
    keep = keep_row[0:1, :]
    gate, up, hidden_grad = sums[:, :units], sums[:, units : 2 * units], sums[:, 2 * units :]
    sig = jax.nn.sigmoid(gate)
    act = gate * sig
    hidden[...] = (act * up * keep).astype(jnp.bfloat16)
    dup = (hidden_grad * act * keep).astype(jnp.bfloat16)
    dgate = (hidden_grad * up * sig * (1.0 + gate * (1.0 - sig)) * keep).astype(jnp.bfloat16)
    up_grad[...] = dup
    gate_grad[...] = dgate
    both[...] = jnp.concatenate((dgate, dup), axis=1)

    def backward(i, carry):
        part = pl.ds(pl.multiple_of(i * STEP, STEP), STEP)
        weights = jnp.concatenate((w_gate[part, :], w_up[part, :]), axis=1)
        out = dot(both[...], weights, NT).astype(jnp.bfloat16)
        term[:, :, part] = out.reshape(blocks, half, STEP)
        return carry

    lax.fori_loop(0, width // STEP, backward, 0)


def middle(keep, group, w_gate, w_up, w_down):
    blocks, pair, width = group.shape
    units = w_gate.shape[1]
    size = blocks * pair // 2
    vmem = pl.BlockSpec(memory_space=pltpu.VMEM)
    grads = jax.ShapeDtypeStruct((size, units), jnp.bfloat16)
    return pl.pallas_call(
        middle_kernel,
        out_shape=(
            jax.ShapeDtypeStruct((blocks, pair // 2, width), jnp.bfloat16),
            grads,
            grads,
            grads,
        ),
        in_specs=[vmem, vmem, vmem, vmem, vmem],
        out_specs=(vmem, vmem, vmem, vmem),
        scratch_shapes=[
            pltpu.VMEM((size, 3 * units), jnp.float32),
            pltpu.VMEM((size, 2 * units), jnp.bfloat16),
        ],
        compiler_params=pltpu.CompilerParams(vmem_limit_bytes=VMEM_LIMIT),
        cost_estimate=pl.CostEstimate(
            flops=10 * size * units * width, bytes_accessed=8 * 2**20, transcendentals=size * units
        ),
    )(keep, group, w_gate, w_up, w_down)


def sum_kernel(parts, out):
    def step(i, carry):
        part = pl.ds(pl.multiple_of(i * STEP, STEP), STEP)
        total = parts[0, :, part].astype(jnp.float32)
        for j in range(1, parts.shape[0]):
            total += parts[j, :, part].astype(jnp.float32)
        out[:, part] = total.astype(jnp.bfloat16)
        return carry

    lax.fori_loop(0, out.shape[1] // STEP, step, 0)


def sum_parts(parts):
    return pl.pallas_call(
        sum_kernel,
        out_shape=jax.ShapeDtypeStruct(parts.shape[1:], jnp.bfloat16),
        in_specs=[pl.BlockSpec(memory_space=pltpu.VMEM)],
        out_specs=pl.BlockSpec(memory_space=pltpu.VMEM),
        compiler_params=pltpu.CompilerParams(vmem_limit_bytes=VMEM_LIMIT),
    )(parts)


def body(x_rows, cot_rows, counts, w_gate, w_up, w_down, kept_blocks, block_rank):
    experts, capacity, width = x_rows.shape[2:]
    my_expert = lax.axis_index(EXPERT)
    picked = jnp.arange(experts, dtype=jnp.int32)[None, :] == my_expert
    own_counts = jnp.sum(jnp.where(picked, counts[:, 0, :], 0), axis=1)
    chooser = compact_matrix(own_counts, capacity)
    back = chooser.reshape(LIVE, experts * capacity).T
    kind = jnp.eye(2, dtype=jnp.bfloat16)
    both = kind[:, None, None, :, None] * chooser[None, :, :, None, :]
    both = both.reshape(2 * LIVE, experts * 2 * capacity)

    slots = jnp.stack((x_rows[0, 0], cot_rows[0, 0]), axis=1)
    keep = (block_rank.reshape(()) < kept_blocks.reshape(())).astype(jnp.float32)
    keep = jnp.broadcast_to(keep, (8, w_gate.shape[2]))
    got = exchange(slots, EXPERT)
    got, both, back, keep = lax.optimization_barrier((got, both, back, keep))
    got = got.reshape(experts * 2 * capacity, width)
    packed = dot(both, got).astype(jnp.bfloat16)
    column = lax.all_gather(packed, "z_hi", axis=0, tiled=True)
    group = exchange(fan_out(column, 16), CHIP_PLANE, WHOLE)
    term, hidden, gate_grad, up_grad = middle(
        keep, group, w_gate[0], w_up[0], w_down[0]
    )
    parts = exchange(term, CHIP_PLANE, WHOLE)
    plane_sum = sum_parts(parts)
    plane_sum, group, hidden, gate_grad, up_grad = lax.optimization_barrier(
        (plane_sum, group, hidden, gate_grad, up_grad)
    )
    parts = exchange(plane_sum.reshape(4, LIVE, width), "z_hi")
    rows = group[:, : 4 * LIVE].reshape(64 * LIVE, width)
    cots = group[:, 4 * LIVE :].reshape(64 * LIVE, width)
    grad_down = dot(hidden, cots, TN).astype(jnp.bfloat16)
    grad_gate = dot(rows, gate_grad, TN).astype(jnp.bfloat16)
    grad_up = dot(rows, up_grad, TN).astype(jnp.bfloat16)
    parts, grad_gate, grad_up, grad_down = lax.optimization_barrier(
        (parts, grad_gate, grad_up, grad_down)
    )
    row_grads = jnp.sum(parts.astype(jnp.float32), axis=0).astype(jnp.bfloat16)
    slot_grads = dot(back, row_grads)
    slot_grads = slot_grads.astype(jnp.bfloat16).reshape(experts, capacity, width)
    grad_rows = exchange(slot_grads, EXPERT)[None, None]
    return (grad_rows, grad_gate[None], grad_up[None], grad_down[None])


def solution(mesh):
    fine = Mesh(np.asarray(mesh.devices).reshape(4, 2, 4, 4, 4), EXPERT + DP)
    in_specs = (
        P(EXPERT, DP, None, None, None),
        P(EXPERT, DP, None, None, None),
        P(None, DP, None),
        P(EXPERT, None, DP),
        P(EXPERT, None, DP),
        P(EXPERT, DP, None),
        P(EXPERT),
        P(EXPERT, DP),
    )
    out_specs = (
        P(EXPERT, DP, None, None, None),
        P(EXPERT, None, DP),
        P(EXPERT, None, DP),
        P(EXPERT, DP, None),
    )
    return jax.shard_map(body, mesh=fine, in_specs=in_specs, out_specs=out_specs, check_vma=False)
```

```python
import jax
import jax.numpy as jnp
import numpy as np
from jax import lax
from jax.experimental import pallas as pl
from jax.experimental.pallas import tpu as pltpu
from jax.sharding import Mesh
from jax.sharding import PartitionSpec as P

LIVE = 4
EXPERT = ("z_lo", "core")
DP = ("z_hi", "x", "y")
STEP = 512
NN = (((1,), (0,)), ((), ()))
NT = (((1,), (1,)), ((), ()))
TN = (((0,), (0,)), ((), ()))
VMEM_LIMIT = 40 * 2**20


def dot(left, right, dims=NN):
    return lax.dot_general(left, right, dims, preferred_element_type=jnp.float32)


def compact_matrix(slot_counts, capacity):
    sources = slot_counts.shape[0]
    earlier = jnp.arange(sources)[None, :] < jnp.arange(sources)[:, None]
    offsets = jnp.sum(jnp.where(earlier, slot_counts[None, :], 0), axis=1)
    within = jnp.arange(capacity, dtype=jnp.int32)[None, :]
    target = jnp.where(within < slot_counts[:, None], offsets[:, None] + within, -1)
    row = jnp.arange(LIVE, dtype=jnp.int32)[:, None, None]
    return (row == target[None]).astype(jnp.bfloat16)


CHIP_PLANE = ("core", "x", "y")
ALONG_X = [[x * 4 + y for x in range(4)] for y in range(4)]
ALONG_Y = [[x * 4 + y for y in range(4)] for x in range(4)]


def per_core(first, second):
    return first + [[16 + place for place in group] for group in second]


FAR = per_core(ALONG_Y, ALONG_X)
WHOLE = per_core([sum(ALONG_X, [])], [sum(ALONG_Y, [])])


CHIP = ("core", "z_hi", "x", "y")


def snake(line):
    return [z * 16 + place for z in range(4) for place in (line[::-1] if z % 2 else line)]


NEAR = [snake(line) for line in ALONG_X] + [[64 + p for p in snake(line)] for line in ALONG_Y]


def exchange(array, axes, groups=None):
    return lax.all_to_all(
        array, axes, split_axis=0, concat_axis=0, axis_index_groups=groups, tiled=True
    )


def order_kernel(line, fan):
    size, width = line.shape
    out = lax.broadcasted_iota(jnp.int32, (size, size), 0)
    z_hi = (out >> 2) & 3
    place = z_hi * 4 + ((out >> 5) ^ (3 * (z_hi & 1)))
    source = place * 8 + ((out >> 4) & 1) * 4 + (out & 3)
    order = (source == lax.broadcasted_iota(jnp.int32, (size, size), 1)).astype(jnp.bfloat16)

    def step(i, carry):
        part = pl.ds(pl.multiple_of(i * STEP, STEP), STEP)
        ordered = dot(order, line[:, part]).astype(jnp.bfloat16).reshape(4, size // 4, STEP)
        for j in range(fan.shape[0]):
            fan[j, :, :, part] = ordered
        return carry

    lax.fori_loop(0, width // STEP, step, 0)


def fan_out(line):
    return pl.pallas_call(
        order_kernel,
        out_shape=jax.ShapeDtypeStruct((4, 4, line.shape[0] // 4, line.shape[1]), jnp.bfloat16),
        in_specs=[pl.BlockSpec(memory_space=pltpu.VMEM)],
        out_specs=pl.BlockSpec(memory_space=pltpu.VMEM),
        compiler_params=pltpu.CompilerParams(vmem_limit_bytes=VMEM_LIMIT),
    )(line)


def middle_kernel(
    keep_row, group, w_gate, w_up, w_down, term, hidden, gate_grad, up_grad, sums, both
):
    blocks, pair, width = group.shape
    half = pair // 2
    size = blocks * half
    units = w_gate.shape[1]
    sums[...] = jnp.zeros_like(sums)

    def forward(i, carry):
        part = pl.ds(pl.multiple_of(i * STEP, STEP), STEP)
        rows = group[:, :half, part].reshape(size, STEP)
        cots = group[:, half:, part].reshape(size, STEP)
        weights = jnp.concatenate((w_gate[part, :], w_up[part, :]), axis=1)
        sums[:, : 2 * units] += dot(rows, weights)
        sums[:, 2 * units :] += dot(cots, w_down[:, part], NT)
        return carry

    lax.fori_loop(0, width // STEP, forward, 0)
    keep = keep_row[0:1, :]
    gate, up, hidden_grad = sums[:, :units], sums[:, units : 2 * units], sums[:, 2 * units :]
    sig = jax.nn.sigmoid(gate)
    act = gate * sig
    hidden[...] = (act * up * keep).astype(jnp.bfloat16)
    dup = (hidden_grad * act * keep).astype(jnp.bfloat16)
    dgate = (hidden_grad * up * sig * (1.0 + gate * (1.0 - sig)) * keep).astype(jnp.bfloat16)
    up_grad[...] = dup
    gate_grad[...] = dgate
    both[...] = jnp.concatenate((dgate, dup), axis=1)

    def backward(i, carry):
        part = pl.ds(pl.multiple_of(i * STEP, STEP), STEP)
        weights = jnp.concatenate((w_gate[part, :], w_up[part, :]), axis=1)
        out = dot(both[...], weights, NT).astype(jnp.bfloat16)
        term[:, :, part] = out.reshape(blocks, half, STEP)
        return carry

    lax.fori_loop(0, width // STEP, backward, 0)


def middle(keep, group, w_gate, w_up, w_down):
    blocks, pair, width = group.shape
    units = w_gate.shape[1]
    size = blocks * pair // 2
    vmem = pl.BlockSpec(memory_space=pltpu.VMEM)
    grads = jax.ShapeDtypeStruct((size, units), jnp.bfloat16)
    return pl.pallas_call(
        middle_kernel,
        out_shape=(
            jax.ShapeDtypeStruct((blocks, pair // 2, width), jnp.bfloat16),
            grads,
            grads,
            grads,
        ),
        in_specs=[vmem, vmem, vmem, vmem, vmem],
        out_specs=(vmem, vmem, vmem, vmem),
        scratch_shapes=[
            pltpu.VMEM((size, 3 * units), jnp.float32),
            pltpu.VMEM((size, 2 * units), jnp.bfloat16),
        ],
        compiler_params=pltpu.CompilerParams(vmem_limit_bytes=VMEM_LIMIT),
        cost_estimate=pl.CostEstimate(
            flops=10 * size * units * width, bytes_accessed=8 * 2**20, transcendentals=size * units
        ),
    )(keep, group, w_gate, w_up, w_down)


def sum_kernel(parts, out):
    def step(i, carry):
        part = pl.ds(pl.multiple_of(i * STEP, STEP), STEP)
        total = parts[0, :, part].astype(jnp.float32)
        for j in range(1, parts.shape[0]):
            total += parts[j, :, part].astype(jnp.float32)
        out[:, part] = total.astype(jnp.bfloat16)
        return carry

    lax.fori_loop(0, out.shape[1] // STEP, step, 0)


def sum_parts(parts):
    return pl.pallas_call(
        sum_kernel,
        out_shape=jax.ShapeDtypeStruct(parts.shape[1:], jnp.bfloat16),
        in_specs=[pl.BlockSpec(memory_space=pltpu.VMEM)],
        out_specs=pl.BlockSpec(memory_space=pltpu.VMEM),
        compiler_params=pltpu.CompilerParams(vmem_limit_bytes=VMEM_LIMIT),
    )(parts)


def body(x_rows, cot_rows, counts, w_gate, w_up, w_down, kept_blocks, block_rank):
    experts, capacity, width = x_rows.shape[2:]
    my_expert = lax.axis_index(EXPERT)
    picked = jnp.arange(experts, dtype=jnp.int32)[None, :] == my_expert
    own_counts = jnp.sum(jnp.where(picked, counts[:, 0, :], 0), axis=1)
    chooser = compact_matrix(own_counts, capacity)
    back = chooser.reshape(LIVE, experts * capacity).T
    kind = jnp.eye(2, dtype=jnp.bfloat16)
    both = kind[:, None, None, :, None] * chooser[None, :, :, None, :]
    both = both.reshape(2 * LIVE, experts * 2 * capacity)

    slots = jnp.stack((x_rows[0, 0], cot_rows[0, 0]), axis=1)
    keep = (block_rank.reshape(()) < kept_blocks.reshape(())).astype(jnp.float32)
    keep = jnp.broadcast_to(keep, (8, w_gate.shape[2]))
    got = exchange(slots, EXPERT)
    got, both, back, keep = lax.optimization_barrier((got, both, back, keep))
    got = got.reshape(experts * 2 * capacity, width)
    packed = dot(both, got).astype(jnp.bfloat16)
    line = lax.all_gather(packed, CHIP, axis=0, tiled=True, axis_index_groups=NEAR)
    group = exchange(fan_out(line), CHIP_PLANE, FAR).reshape(16, 8 * LIVE, width)
    term, hidden, gate_grad, up_grad = middle(
        keep, group, w_gate[0], w_up[0], w_down[0]
    )
    parts = exchange(term, CHIP_PLANE, WHOLE)
    plane_sum = sum_parts(parts)
    plane_sum, group, hidden, gate_grad, up_grad = lax.optimization_barrier(
        (plane_sum, group, hidden, gate_grad, up_grad)
    )
    parts = exchange(plane_sum.reshape(4, LIVE, width), "z_hi")
    rows = group[:, : 4 * LIVE].reshape(64 * LIVE, width)
    cots = group[:, 4 * LIVE :].reshape(64 * LIVE, width)
    grad_down = dot(hidden, cots, TN).astype(jnp.bfloat16)
    grad_gate = dot(rows, gate_grad, TN).astype(jnp.bfloat16)
    grad_up = dot(rows, up_grad, TN).astype(jnp.bfloat16)
    parts, grad_gate, grad_up, grad_down = lax.optimization_barrier(
        (parts, grad_gate, grad_up, grad_down)
    )
    row_grads = jnp.sum(parts.astype(jnp.float32), axis=0).astype(jnp.bfloat16)
    slot_grads = dot(back, row_grads)
    slot_grads = slot_grads.astype(jnp.bfloat16).reshape(experts, capacity, width)
    grad_rows = exchange(slot_grads, EXPERT)[None, None]
    return (grad_rows, grad_gate[None], grad_up[None], grad_down[None])


def solution(mesh):
    fine = Mesh(np.asarray(mesh.devices).reshape(4, 2, 4, 4, 4), EXPERT + DP)
    in_specs = (
        P(EXPERT, DP, None, None, None),
        P(EXPERT, DP, None, None, None),
        P(None, DP, None),
        P(EXPERT, None, DP),
        P(EXPERT, None, DP),
        P(EXPERT, DP, None),
        P(EXPERT),
        P(EXPERT, DP),
    )
    out_specs = (
        P(EXPERT, DP, None, None, None),
        P(EXPERT, None, DP),
        P(EXPERT, None, DP),
        P(EXPERT, DP, None),
    )
    return jax.shard_map(body, mesh=fine, in_specs=in_specs, out_specs=out_specs, check_vma=False)
```

```python
import jax
import jax.numpy as jnp
import numpy as np
from jax import lax
from jax.experimental import pallas as pl
from jax.experimental.pallas import tpu as pltpu
from jax.sharding import Mesh
from jax.sharding import PartitionSpec as P

LIVE = 4
EXPERT = ("z_lo", "core")
DP = ("z_hi", "x", "y")
STEP = 512
NN = (((1,), (0,)), ((), ()))
NT = (((1,), (1,)), ((), ()))
TN = (((0,), (0,)), ((), ()))
VMEM_LIMIT = 40 * 2**20


def dot(left, right, dims=NN):
    return lax.dot_general(left, right, dims, preferred_element_type=jnp.float32)


def compact_matrix(slot_counts, capacity):
    sources = slot_counts.shape[0]
    earlier = jnp.arange(sources)[None, :] < jnp.arange(sources)[:, None]
    offsets = jnp.sum(jnp.where(earlier, slot_counts[None, :], 0), axis=1)
    within = jnp.arange(capacity, dtype=jnp.int32)[None, :]
    target = jnp.where(within < slot_counts[:, None], offsets[:, None] + within, -1)
    row = jnp.arange(LIVE, dtype=jnp.int32)[:, None, None]
    return (row == target[None]).astype(jnp.bfloat16)


CHIP_PLANE = ("core", "x", "y")
ALONG_X = [[x * 4 + y for x in range(4)] for y in range(4)]
ALONG_Y = [[x * 4 + y for y in range(4)] for x in range(4)]


def per_core(first, second):
    return first + [[16 + place for place in group] for group in second]


NEAR = per_core(ALONG_X, ALONG_Y)
FAR = per_core(ALONG_Y, ALONG_X)
WHOLE = per_core([sum(ALONG_X, [])], [sum(ALONG_Y, [])])


def exchange(array, axes, groups=None):
    return lax.all_to_all(
        array, axes, split_axis=0, concat_axis=0, axis_index_groups=groups, tiled=True
    )


def order_kernel(column, fan):
    size = column.shape[0]
    out = lax.broadcasted_iota(jnp.int32, (size, size), 0)
    source = ((out & 15) >> 2) * 8 + (out >> 4) * 4 + (out & 3)
    order = (source == lax.broadcasted_iota(jnp.int32, (size, size), 1)).astype(jnp.bfloat16)
    ordered = dot(order, column[...]).astype(jnp.bfloat16)
    for i in range(fan.shape[0]):
        fan[i] = ordered


def copy_kernel(block, fan):
    for i in range(fan.shape[0]):
        fan[i] = block[...]


def fan_out(kernel, block, receivers):
    return pl.pallas_call(
        kernel,
        out_shape=jax.ShapeDtypeStruct((receivers,) + block.shape, jnp.bfloat16),
        in_specs=[pl.BlockSpec(memory_space=pltpu.VMEM)],
        out_specs=pl.BlockSpec(memory_space=pltpu.VMEM),
        compiler_params=pltpu.CompilerParams(vmem_limit_bytes=VMEM_LIMIT),
    )(block)


def middle_kernel(
    keep_row, group, w_gate, w_up, w_down, term, hidden, gate_grad, up_grad, sums, both
):
    blocks, pair, width = group.shape
    half = pair // 2
    size = blocks * half
    units = w_gate.shape[1]
    sums[...] = jnp.zeros_like(sums)

    def forward(i, carry):
        part = pl.ds(pl.multiple_of(i * STEP, STEP), STEP)
        rows = group[:, :half, part].reshape(size, STEP)
        cots = group[:, half:, part].reshape(size, STEP)
        weights = jnp.concatenate((w_gate[part, :], w_up[part, :]), axis=1)
        sums[:, : 2 * units] += dot(rows, weights)
        sums[:, 2 * units :] += dot(cots, w_down[:, part], NT)
        return carry

    lax.fori_loop(0, width // STEP, forward, 0)
    keep = keep_row[0:1, :]
    gate, up, hidden_grad = sums[:, :units], sums[:, units : 2 * units], sums[:, 2 * units :]
    sig = jax.nn.sigmoid(gate)
    act = gate * sig
    hidden[...] = (act * up * keep).astype(jnp.bfloat16)
    dup = (hidden_grad * act * keep).astype(jnp.bfloat16)
    dgate = (hidden_grad * up * sig * (1.0 + gate * (1.0 - sig)) * keep).astype(jnp.bfloat16)
    up_grad[...] = dup
    gate_grad[...] = dgate
    both[...] = jnp.concatenate((dgate, dup), axis=1)

    def backward(i, carry):
        part = pl.ds(pl.multiple_of(i * STEP, STEP), STEP)
        weights = jnp.concatenate((w_gate[part, :], w_up[part, :]), axis=1)
        out = dot(both[...], weights, NT).astype(jnp.bfloat16)
        term[:, :, part] = out.reshape(blocks, half, STEP)
        return carry

    lax.fori_loop(0, width // STEP, backward, 0)


def middle(keep, group, w_gate, w_up, w_down):
    blocks, pair, width = group.shape
    units = w_gate.shape[1]
    size = blocks * pair // 2
    vmem = pl.BlockSpec(memory_space=pltpu.VMEM)
    grads = jax.ShapeDtypeStruct((size, units), jnp.bfloat16)
    return pl.pallas_call(
        middle_kernel,
        out_shape=(
            jax.ShapeDtypeStruct((blocks, pair // 2, width), jnp.bfloat16),
            grads,
            grads,
            grads,
        ),
        in_specs=[vmem, vmem, vmem, vmem, vmem],
        out_specs=(vmem, vmem, vmem, vmem),
        scratch_shapes=[
            pltpu.VMEM((size, 3 * units), jnp.float32),
            pltpu.VMEM((size, 2 * units), jnp.bfloat16),
        ],
        compiler_params=pltpu.CompilerParams(vmem_limit_bytes=VMEM_LIMIT),
        cost_estimate=pl.CostEstimate(
            flops=10 * size * units * width, bytes_accessed=8 * 2**20, transcendentals=size * units
        ),
    )(keep, group, w_gate, w_up, w_down)


def sum_kernel(parts, out):
    def step(i, carry):
        part = pl.ds(pl.multiple_of(i * STEP, STEP), STEP)
        total = parts[0, :, part].astype(jnp.float32)
        for j in range(1, parts.shape[0]):
            total += parts[j, :, part].astype(jnp.float32)
        out[:, part] = total.astype(jnp.bfloat16)
        return carry

    lax.fori_loop(0, out.shape[1] // STEP, step, 0)


def sum_parts(parts):
    return pl.pallas_call(
        sum_kernel,
        out_shape=jax.ShapeDtypeStruct(parts.shape[1:], jnp.bfloat16),
        in_specs=[pl.BlockSpec(memory_space=pltpu.VMEM)],
        out_specs=pl.BlockSpec(memory_space=pltpu.VMEM),
        compiler_params=pltpu.CompilerParams(vmem_limit_bytes=VMEM_LIMIT),
    )(parts)


def body(x_rows, cot_rows, counts, w_gate, w_up, w_down, kept_blocks, block_rank):
    experts, capacity, width = x_rows.shape[2:]
    my_expert = lax.axis_index(EXPERT)
    picked = jnp.arange(experts, dtype=jnp.int32)[None, :] == my_expert
    own_counts = jnp.sum(jnp.where(picked, counts[:, 0, :], 0), axis=1)
    chooser = compact_matrix(own_counts, capacity)
    back = chooser.reshape(LIVE, experts * capacity).T
    kind = jnp.eye(2, dtype=jnp.bfloat16)
    both = kind[:, None, None, :, None] * chooser[None, :, :, None, :]
    both = both.reshape(2 * LIVE, experts * 2 * capacity)

    slots = jnp.stack((x_rows[0, 0], cot_rows[0, 0]), axis=1)
    keep = (block_rank.reshape(()) < kept_blocks.reshape(())).astype(jnp.float32)
    keep = jnp.broadcast_to(keep, (8, w_gate.shape[2]))
    got = exchange(slots, EXPERT)
    got, both, back, keep = lax.optimization_barrier((got, both, back, keep))
    got = got.reshape(experts * 2 * capacity, width)
    packed = dot(both, got).astype(jnp.bfloat16)
    column = lax.all_gather(packed, "z_hi", axis=0, tiled=True)
    column = fan_out(order_kernel, column, 1)[0]
    line = lax.all_gather(column, CHIP_PLANE, axis=0, axis_index_groups=NEAR)
    group = exchange(fan_out(copy_kernel, line, 4), CHIP_PLANE, FAR)
    group = group.reshape(16, 8 * LIVE, width)
    term, hidden, gate_grad, up_grad = middle(
        keep, group, w_gate[0], w_up[0], w_down[0]
    )
    parts = exchange(term, CHIP_PLANE, WHOLE)
    plane_sum = sum_parts(parts)
    plane_sum, group, hidden, gate_grad, up_grad = lax.optimization_barrier(
        (plane_sum, group, hidden, gate_grad, up_grad)
    )
    parts = exchange(plane_sum.reshape(4, LIVE, width), "z_hi")
    rows = group[:, : 4 * LIVE].reshape(64 * LIVE, width)
    cots = group[:, 4 * LIVE :].reshape(64 * LIVE, width)
    grad_down = dot(hidden, cots, TN).astype(jnp.bfloat16)
    grad_gate = dot(rows, gate_grad, TN).astype(jnp.bfloat16)
    grad_up = dot(rows, up_grad, TN).astype(jnp.bfloat16)
    parts, grad_gate, grad_up, grad_down = lax.optimization_barrier(
        (parts, grad_gate, grad_up, grad_down)
    )
    row_grads = jnp.sum(parts.astype(jnp.float32), axis=0).astype(jnp.bfloat16)
    slot_grads = dot(back, row_grads)
    slot_grads = slot_grads.astype(jnp.bfloat16).reshape(experts, capacity, width)
    grad_rows = exchange(slot_grads, EXPERT)[None, None]
    return (grad_rows, grad_gate[None], grad_up[None], grad_down[None])


def solution(mesh):
    fine = Mesh(np.asarray(mesh.devices).reshape(4, 2, 4, 4, 4), EXPERT + DP)
    in_specs = (
        P(EXPERT, DP, None, None, None),
        P(EXPERT, DP, None, None, None),
        P(None, DP, None),
        P(EXPERT, None, DP),
        P(EXPERT, None, DP),
        P(EXPERT, DP, None),
        P(EXPERT),
        P(EXPERT, DP),
    )
    out_specs = (
        P(EXPERT, DP, None, None, None),
        P(EXPERT, None, DP),
        P(EXPERT, None, DP),
        P(EXPERT, DP, None),
    )
    return jax.shard_map(body, mesh=fine, in_specs=in_specs, out_specs=out_specs, check_vma=False)
```

```python
import jax
import jax.numpy as jnp
import numpy as np
from jax import lax
from jax.experimental import pallas as pl
from jax.experimental.pallas import tpu as pltpu
from jax.sharding import Mesh
from jax.sharding import PartitionSpec as P

LIVE = 4
EXPERT = ("z_lo", "core")
DP = ("z_hi", "x", "y")
STEP = 512
NN = (((1,), (0,)), ((), ()))
NT = (((1,), (1,)), ((), ()))
TN = (((0,), (0,)), ((), ()))
VMEM_LIMIT = 40 * 2**20


def dot(left, right, dims=NN):
    return lax.dot_general(left, right, dims, preferred_element_type=jnp.float32)


def compact_matrix(slot_counts, capacity):
    sources = slot_counts.shape[0]
    earlier = jnp.arange(sources)[None, :] < jnp.arange(sources)[:, None]
    offsets = jnp.sum(jnp.where(earlier, slot_counts[None, :], 0), axis=1)
    within = jnp.arange(capacity, dtype=jnp.int32)[None, :]
    target = jnp.where(within < slot_counts[:, None], offsets[:, None] + within, -1)
    row = jnp.arange(LIVE, dtype=jnp.int32)[:, None, None]
    return (row == target[None]).astype(jnp.bfloat16)


CHIP_PLANE = ("core", "x", "y")
ALONG_X = [[x * 4 + y for x in range(4)] for y in range(4)]
ALONG_Y = [[x * 4 + y for y in range(4)] for x in range(4)]


def per_core(first, second):
    return first + [[16 + place for place in group] for group in second]


NEAR = per_core(ALONG_X, ALONG_Y)
FAR = per_core(ALONG_Y, ALONG_X)
WHOLE = per_core([sum(ALONG_X, [])], [sum(ALONG_Y, [])])


def exchange(array, axes, groups=None):
    return lax.all_to_all(
        array, axes, split_axis=0, concat_axis=0, axis_index_groups=groups, tiled=True
    )


def pair_kernel(rows, cots, pairs, sems):
    copies = [
        pltpu.make_async_copy(source, pairs.at[:, i], sems.at[i])
        for i, source in enumerate((rows, cots))
    ]
    for copy in copies:
        copy.start()
    for copy in copies:
        copy.wait()


def pair_up(rows, cots):
    anywhere = pl.BlockSpec(memory_space=pl.ANY)
    return pl.pallas_call(
        pair_kernel,
        out_shape=jax.ShapeDtypeStruct((rows.shape[0], 2) + rows.shape[1:], jnp.bfloat16),
        in_specs=[anywhere, anywhere],
        out_specs=anywhere,
        scratch_shapes=[pltpu.SemaphoreType.DMA((2,))],
    )(rows, cots)


def order_kernel(column, fan):
    size = column.shape[0]
    out = lax.broadcasted_iota(jnp.int32, (size, size), 0)
    source = ((out & 15) >> 2) * 8 + (out >> 4) * 4 + (out & 3)
    order = (source == lax.broadcasted_iota(jnp.int32, (size, size), 1)).astype(jnp.bfloat16)
    ordered = dot(order, column[...]).astype(jnp.bfloat16)
    for i in range(fan.shape[0]):
        fan[i] = ordered


def copy_kernel(block, fan):
    for i in range(fan.shape[0]):
        fan[i] = block[...]


def fan_out(kernel, block, receivers):
    return pl.pallas_call(
        kernel,
        out_shape=jax.ShapeDtypeStruct((receivers,) + block.shape, jnp.bfloat16),
        in_specs=[pl.BlockSpec(memory_space=pltpu.VMEM)],
        out_specs=pl.BlockSpec(memory_space=pltpu.VMEM),
        compiler_params=pltpu.CompilerParams(vmem_limit_bytes=VMEM_LIMIT),
    )(block)


def middle_kernel(
    keep_row, group, w_gate, w_up, w_down, term, hidden, gate_grad, up_grad, sums, both
):
    blocks, pair, width = group.shape
    half = pair // 2
    size = blocks * half
    units = w_gate.shape[1]
    sums[...] = jnp.zeros_like(sums)

    def forward(i, carry):
        part = pl.ds(pl.multiple_of(i * STEP, STEP), STEP)
        rows = group[:, :half, part].reshape(size, STEP)
        cots = group[:, half:, part].reshape(size, STEP)
        weights = jnp.concatenate((w_gate[part, :], w_up[part, :]), axis=1)
        sums[:, : 2 * units] += dot(rows, weights)
        sums[:, 2 * units :] += dot(cots, w_down[:, part], NT)
        return carry

    lax.fori_loop(0, width // STEP, forward, 0)
    keep = keep_row[0:1, :]
    gate, up, hidden_grad = sums[:, :units], sums[:, units : 2 * units], sums[:, 2 * units :]
    sig = jax.nn.sigmoid(gate)
    act = gate * sig
    hidden[...] = (act * up * keep).astype(jnp.bfloat16)
    dup = (hidden_grad * act * keep).astype(jnp.bfloat16)
    dgate = (hidden_grad * up * sig * (1.0 + gate * (1.0 - sig)) * keep).astype(jnp.bfloat16)
    up_grad[...] = dup
    gate_grad[...] = dgate
    both[...] = jnp.concatenate((dgate, dup), axis=1)

    def backward(i, carry):
        part = pl.ds(pl.multiple_of(i * STEP, STEP), STEP)
        weights = jnp.concatenate((w_gate[part, :], w_up[part, :]), axis=1)
        out = dot(both[...], weights, NT).astype(jnp.bfloat16)
        term[:, :, part] = out.reshape(blocks, half, STEP)
        return carry

    lax.fori_loop(0, width // STEP, backward, 0)


def middle(keep, group, w_gate, w_up, w_down):
    blocks, pair, width = group.shape
    units = w_gate.shape[1]
    size = blocks * pair // 2
    vmem = pl.BlockSpec(memory_space=pltpu.VMEM)
    grads = jax.ShapeDtypeStruct((size, units), jnp.bfloat16)
    return pl.pallas_call(
        middle_kernel,
        out_shape=(
            jax.ShapeDtypeStruct((blocks, pair // 2, width), jnp.bfloat16),
            grads,
            grads,
            grads,
        ),
        in_specs=[vmem, vmem, vmem, vmem, vmem],
        out_specs=(vmem, vmem, vmem, vmem),
        scratch_shapes=[
            pltpu.VMEM((size, 3 * units), jnp.float32),
            pltpu.VMEM((size, 2 * units), jnp.bfloat16),
        ],
        compiler_params=pltpu.CompilerParams(vmem_limit_bytes=VMEM_LIMIT),
        cost_estimate=pl.CostEstimate(
            flops=10 * size * units * width, bytes_accessed=8 * 2**20, transcendentals=size * units
        ),
    )(keep, group, w_gate, w_up, w_down)


def sum_kernel(parts, out):
    def step(i, carry):
        part = pl.ds(pl.multiple_of(i * STEP, STEP), STEP)
        total = parts[0, :, part].astype(jnp.float32)
        for j in range(1, parts.shape[0]):
            total += parts[j, :, part].astype(jnp.float32)
        out[:, part] = total.astype(jnp.bfloat16)
        return carry

    lax.fori_loop(0, out.shape[1] // STEP, step, 0)


def sum_parts(parts):
    return pl.pallas_call(
        sum_kernel,
        out_shape=jax.ShapeDtypeStruct(parts.shape[1:], jnp.bfloat16),
        in_specs=[pl.BlockSpec(memory_space=pltpu.VMEM)],
        out_specs=pl.BlockSpec(memory_space=pltpu.VMEM),
        compiler_params=pltpu.CompilerParams(vmem_limit_bytes=VMEM_LIMIT),
    )(parts)


def body(x_rows, cot_rows, counts, w_gate, w_up, w_down, kept_blocks, block_rank):
    experts, capacity, width = x_rows.shape[2:]
    my_expert = lax.axis_index(EXPERT)
    picked = jnp.arange(experts, dtype=jnp.int32)[None, :] == my_expert
    own_counts = jnp.sum(jnp.where(picked, counts[:, 0, :], 0), axis=1)
    chooser = compact_matrix(own_counts, capacity)
    back = chooser.reshape(LIVE, experts * capacity).T
    kind = jnp.eye(2, dtype=jnp.bfloat16)
    both = kind[:, None, None, :, None] * chooser[None, :, :, None, :]
    both = both.reshape(2 * LIVE, experts * 2 * capacity)

    slots = pair_up(x_rows[0, 0], cot_rows[0, 0])
    keep = (block_rank.reshape(()) < kept_blocks.reshape(())).astype(jnp.float32)
    keep = jnp.broadcast_to(keep, (8, w_gate.shape[2]))
    got = exchange(slots, EXPERT)
    got, both, back, keep = lax.optimization_barrier((got, both, back, keep))
    got = got.reshape(experts * 2 * capacity, width)
    packed = dot(both, got).astype(jnp.bfloat16)
    column = lax.all_gather(packed, "z_hi", axis=0, tiled=True)
    line = exchange(fan_out(order_kernel, column, 4), CHIP_PLANE, NEAR)
    group = exchange(fan_out(copy_kernel, line, 4), CHIP_PLANE, FAR)
    group = group.reshape(16, 8 * LIVE, width)
    term, hidden, gate_grad, up_grad = middle(
        keep, group, w_gate[0], w_up[0], w_down[0]
    )
    parts = exchange(term, CHIP_PLANE, WHOLE)
    plane_sum = sum_parts(parts)
    plane_sum, group, hidden, gate_grad, up_grad = lax.optimization_barrier(
        (plane_sum, group, hidden, gate_grad, up_grad)
    )
    parts = exchange(plane_sum.reshape(4, LIVE, width), "z_hi")
    rows = group[:, : 4 * LIVE].reshape(64 * LIVE, width)
    cots = group[:, 4 * LIVE :].reshape(64 * LIVE, width)
    grad_down = dot(hidden, cots, TN).astype(jnp.bfloat16)
    grad_gate = dot(rows, gate_grad, TN).astype(jnp.bfloat16)
    grad_up = dot(rows, up_grad, TN).astype(jnp.bfloat16)
    parts, grad_gate, grad_up, grad_down = lax.optimization_barrier(
        (parts, grad_gate, grad_up, grad_down)
    )
    row_grads = jnp.sum(parts.astype(jnp.float32), axis=0).astype(jnp.bfloat16)
    slot_grads = dot(back, row_grads)
    slot_grads = slot_grads.astype(jnp.bfloat16).reshape(experts, capacity, width)
    grad_rows = exchange(slot_grads, EXPERT)[None, None]
    return (grad_rows, grad_gate[None], grad_up[None], grad_down[None])


def solution(mesh):
    fine = Mesh(np.asarray(mesh.devices).reshape(4, 2, 4, 4, 4), EXPERT + DP)
    in_specs = (
        P(EXPERT, DP, None, None, None),
        P(EXPERT, DP, None, None, None),
        P(None, DP, None),
        P(EXPERT, None, DP),
        P(EXPERT, None, DP),
        P(EXPERT, DP, None),
        P(EXPERT),
        P(EXPERT, DP),
    )
    out_specs = (
        P(EXPERT, DP, None, None, None),
        P(EXPERT, None, DP),
        P(EXPERT, None, DP),
        P(EXPERT, DP, None),
    )
    return jax.shard_map(body, mesh=fine, in_specs=in_specs, out_specs=out_specs, check_vma=False)
```

```python
import jax
import jax.numpy as jnp
import numpy as np
from jax import lax
from jax.experimental import pallas as pl
from jax.experimental.pallas import tpu as pltpu
from jax.sharding import Mesh
from jax.sharding import PartitionSpec as P

LIVE = 4
EXPERT = ("z_lo", "core")
DP = ("z_hi", "x", "y")
STEP = 512
NN = (((1,), (0,)), ((), ()))
NT = (((1,), (1,)), ((), ()))
TN = (((0,), (0,)), ((), ()))
VMEM_LIMIT = 40 * 2**20


def dot(left, right, dims=NN):
    return lax.dot_general(left, right, dims, preferred_element_type=jnp.float32)


def compact_matrix(slot_counts, capacity):
    sources = slot_counts.shape[0]
    earlier = jnp.arange(sources)[None, :] < jnp.arange(sources)[:, None]
    offsets = jnp.sum(jnp.where(earlier, slot_counts[None, :], 0), axis=1)
    within = jnp.arange(capacity, dtype=jnp.int32)[None, :]
    target = jnp.where(within < slot_counts[:, None], offsets[:, None] + within, -1)
    row = jnp.arange(LIVE, dtype=jnp.int32)[:, None, None]
    return (row == target[None]).astype(jnp.bfloat16)


CHIP_PLANE = ("core", "x", "y")
ALONG_X = [[x * 4 + y for x in range(4)] for y in range(4)]
ALONG_Y = [[x * 4 + y for y in range(4)] for x in range(4)]


def per_core(first, second):
    return first + [[16 + place for place in group] for group in second]


NEAR = per_core(ALONG_Y, ALONG_X)
FAR = per_core(ALONG_X, ALONG_Y)
WHOLE = per_core([sum(ALONG_Y, [])], [sum(ALONG_X, [])])


def exchange(array, axes, groups=None):
    return lax.all_to_all(
        array, axes, split_axis=0, concat_axis=0, axis_index_groups=groups, tiled=True
    )


def order_kernel(column, fan):
    size = column.shape[0]
    out = lax.broadcasted_iota(jnp.int32, (size, size), 0)
    source = ((out & 15) >> 2) * 8 + (out >> 4) * 4 + (out & 3)
    order = (source == lax.broadcasted_iota(jnp.int32, (size, size), 1)).astype(jnp.bfloat16)
    ordered = dot(order, column[...]).astype(jnp.bfloat16)
    for i in range(fan.shape[0]):
        fan[i] = ordered


def copy_kernel(block, fan):
    for i in range(fan.shape[0]):
        fan[i] = block[...]


def fan_out(kernel, block, receivers):
    return pl.pallas_call(
        kernel,
        out_shape=jax.ShapeDtypeStruct((receivers,) + block.shape, jnp.bfloat16),
        in_specs=[pl.BlockSpec(memory_space=pltpu.VMEM)],
        out_specs=pl.BlockSpec(memory_space=pltpu.VMEM),
        compiler_params=pltpu.CompilerParams(vmem_limit_bytes=VMEM_LIMIT),
    )(block)


def middle_kernel(
    keep_row, group, w_gate, w_up, w_down, term, hidden, gate_grad, up_grad, sums, both
):
    blocks, pair, width = group.shape
    half = pair // 2
    size = blocks * half
    units = w_gate.shape[1]
    sums[...] = jnp.zeros_like(sums)

    def forward(i, carry):
        part = pl.ds(pl.multiple_of(i * STEP, STEP), STEP)
        rows = group[:, :half, part].reshape(size, STEP)
        cots = group[:, half:, part].reshape(size, STEP)
        weights = jnp.concatenate((w_gate[part, :], w_up[part, :]), axis=1)
        sums[:, : 2 * units] += dot(rows, weights)
        sums[:, 2 * units :] += dot(cots, w_down[:, part], NT)
        return carry

    lax.fori_loop(0, width // STEP, forward, 0)
    keep = keep_row[0:1, :]
    gate, up, hidden_grad = sums[:, :units], sums[:, units : 2 * units], sums[:, 2 * units :]
    sig = jax.nn.sigmoid(gate)
    act = gate * sig
    hidden[...] = (act * up * keep).astype(jnp.bfloat16)
    dup = (hidden_grad * act * keep).astype(jnp.bfloat16)
    dgate = (hidden_grad * up * sig * (1.0 + gate * (1.0 - sig)) * keep).astype(jnp.bfloat16)
    up_grad[...] = dup
    gate_grad[...] = dgate
    both[...] = jnp.concatenate((dgate, dup), axis=1)

    def backward(i, carry):
        part = pl.ds(pl.multiple_of(i * STEP, STEP), STEP)
        weights = jnp.concatenate((w_gate[part, :], w_up[part, :]), axis=1)
        out = dot(both[...], weights, NT).astype(jnp.bfloat16)
        term[:, :, part] = out.reshape(blocks, half, STEP)
        return carry

    lax.fori_loop(0, width // STEP, backward, 0)


def middle(keep, group, w_gate, w_up, w_down):
    blocks, pair, width = group.shape
    units = w_gate.shape[1]
    size = blocks * pair // 2
    vmem = pl.BlockSpec(memory_space=pltpu.VMEM)
    grads = jax.ShapeDtypeStruct((size, units), jnp.bfloat16)
    return pl.pallas_call(
        middle_kernel,
        out_shape=(
            jax.ShapeDtypeStruct((blocks, pair // 2, width), jnp.bfloat16),
            grads,
            grads,
            grads,
        ),
        in_specs=[vmem, vmem, vmem, vmem, vmem],
        out_specs=(vmem, vmem, vmem, vmem),
        scratch_shapes=[
            pltpu.VMEM((size, 3 * units), jnp.float32),
            pltpu.VMEM((size, 2 * units), jnp.bfloat16),
        ],
        compiler_params=pltpu.CompilerParams(vmem_limit_bytes=VMEM_LIMIT),
        cost_estimate=pl.CostEstimate(
            flops=10 * size * units * width, bytes_accessed=8 * 2**20, transcendentals=size * units
        ),
    )(keep, group, w_gate, w_up, w_down)


def sum_kernel(parts, out):
    def step(i, carry):
        part = pl.ds(pl.multiple_of(i * STEP, STEP), STEP)
        total = parts[0, :, part].astype(jnp.float32)
        for j in range(1, parts.shape[0]):
            total += parts[j, :, part].astype(jnp.float32)
        for j in range(out.shape[0]):
            out[j, :, part] = total[j * LIVE : (j + 1) * LIVE].astype(jnp.bfloat16)
        return carry

    lax.fori_loop(0, out.shape[2] // STEP, step, 0)


def sum_parts(parts):
    return pl.pallas_call(
        sum_kernel,
        out_shape=jax.ShapeDtypeStruct((4, LIVE, parts.shape[2]), jnp.bfloat16),
        in_specs=[pl.BlockSpec(memory_space=pltpu.VMEM)],
        out_specs=pl.BlockSpec(memory_space=pltpu.VMEM),
        compiler_params=pltpu.CompilerParams(vmem_limit_bytes=VMEM_LIMIT),
    )(parts)


def body(x_rows, cot_rows, counts, w_gate, w_up, w_down, kept_blocks, block_rank):
    experts, capacity, width = x_rows.shape[2:]
    my_expert = lax.axis_index(EXPERT)
    picked = jnp.arange(experts, dtype=jnp.int32)[None, :] == my_expert
    own_counts = jnp.sum(jnp.where(picked, counts[:, 0, :], 0), axis=1)
    chooser = compact_matrix(own_counts, capacity)
    back = chooser.reshape(LIVE, experts * capacity).T
    kind = jnp.eye(2, dtype=jnp.bfloat16)
    both = kind[:, None, None, :, None] * chooser[None, :, :, None, :]
    both = both.reshape(2 * LIVE, experts * 2 * capacity)

    slots = jnp.stack((x_rows[0, 0], cot_rows[0, 0]), axis=1)
    keep = (block_rank.reshape(()) < kept_blocks.reshape(())).astype(jnp.float32)
    keep = jnp.broadcast_to(keep, (8, w_gate.shape[2]))
    got = exchange(slots, EXPERT)
    got, both, back, keep = lax.optimization_barrier((got, both, back, keep))
    got = got.reshape(experts * 2 * capacity, width)
    packed = dot(both, got).astype(jnp.bfloat16)
    column = lax.all_gather(packed, "z_hi", axis=0, tiled=True)
    line = exchange(fan_out(order_kernel, column, 4), CHIP_PLANE, NEAR)
    group = exchange(fan_out(copy_kernel, line, 4), CHIP_PLANE, FAR)
    group = group.reshape(16, 8 * LIVE, width)
    term, hidden, gate_grad, up_grad = middle(
        keep, group, w_gate[0], w_up[0], w_down[0]
    )
    parts = exchange(term, CHIP_PLANE, WHOLE)
    plane_sum = sum_parts(parts)
    plane_sum, group, hidden, gate_grad, up_grad = lax.optimization_barrier(
        (plane_sum, group, hidden, gate_grad, up_grad)
    )
    parts = exchange(plane_sum, "z_hi")
    rows = group[:, : 4 * LIVE].reshape(64 * LIVE, width)
    cots = group[:, 4 * LIVE :].reshape(64 * LIVE, width)
    grad_down = dot(hidden, cots, TN).astype(jnp.bfloat16)
    grad_gate = dot(rows, gate_grad, TN).astype(jnp.bfloat16)
    grad_up = dot(rows, up_grad, TN).astype(jnp.bfloat16)
    parts, grad_gate, grad_up, grad_down = lax.optimization_barrier(
        (parts, grad_gate, grad_up, grad_down)
    )
    row_grads = jnp.sum(parts.astype(jnp.float32), axis=0).astype(jnp.bfloat16)
    slot_grads = dot(back, row_grads)
    slot_grads = slot_grads.astype(jnp.bfloat16).reshape(experts, capacity, width)
    grad_rows = exchange(slot_grads, EXPERT)[None, None]
    return (grad_rows, grad_gate[None], grad_up[None], grad_down[None])


def solution(mesh):
    fine = Mesh(np.asarray(mesh.devices).reshape(4, 2, 4, 4, 4), EXPERT + DP)
    in_specs = (
        P(EXPERT, DP, None, None, None),
        P(EXPERT, DP, None, None, None),
        P(None, DP, None),
        P(EXPERT, None, DP),
        P(EXPERT, None, DP),
        P(EXPERT, DP, None),
        P(EXPERT),
        P(EXPERT, DP),
    )
    out_specs = (
        P(EXPERT, DP, None, None, None),
        P(EXPERT, None, DP),
        P(EXPERT, None, DP),
        P(EXPERT, DP, None),
    )
    return jax.shard_map(body, mesh=fine, in_specs=in_specs, out_specs=out_specs, check_vma=False)
```

```python
import jax
import jax.numpy as jnp
import numpy as np
from jax import lax
from jax.experimental import pallas as pl
from jax.experimental.pallas import tpu as pltpu
from jax.sharding import Mesh
from jax.sharding import PartitionSpec as P

LIVE = 4
EXPERT = ("z_lo", "core")
DP = ("z_hi", "x", "y")
STEP = 512
NN = (((1,), (0,)), ((), ()))
NT = (((1,), (1,)), ((), ()))
TN = (((0,), (0,)), ((), ()))
VMEM_LIMIT = 40 * 2**20


def dot(left, right, dims=NN):
    return lax.dot_general(left, right, dims, preferred_element_type=jnp.float32)


def compact_matrix(slot_counts, capacity):
    sources = slot_counts.shape[0]
    earlier = jnp.arange(sources)[None, :] < jnp.arange(sources)[:, None]
    offsets = jnp.sum(jnp.where(earlier, slot_counts[None, :], 0), axis=1)
    within = jnp.arange(capacity, dtype=jnp.int32)[None, :]
    target = jnp.where(within < slot_counts[:, None], offsets[:, None] + within, -1)
    row = jnp.arange(LIVE, dtype=jnp.int32)[:, None, None]
    return (row == target[None]).astype(jnp.bfloat16)


CHIP_PLANE = ("core", "x", "y")
ALONG_X = [[x * 4 + y for x in range(4)] for y in range(4)]
ALONG_Y = [[x * 4 + y for y in range(4)] for x in range(4)]


def per_core(first, second):
    return first + [[16 + place for place in group] for group in second]


NEAR = per_core(ALONG_Y, ALONG_X)
FAR = per_core(ALONG_X, ALONG_Y)
WHOLE = per_core([sum(ALONG_Y, [])], [sum(ALONG_X, [])])


def exchange(array, axes, groups=None):
    return lax.all_to_all(
        array, axes, split_axis=0, concat_axis=0, axis_index_groups=groups, tiled=True
    )


def order_kernel(column, fan):
    size = column.shape[0]
    out = lax.broadcasted_iota(jnp.int32, (size, size), 0)
    source = ((out & 15) >> 2) * 8 + (out >> 4) * 4 + (out & 3)
    order = (source == lax.broadcasted_iota(jnp.int32, (size, size), 1)).astype(jnp.bfloat16)
    ordered = dot(order, column[...]).astype(jnp.bfloat16)
    for i in range(fan.shape[0]):
        fan[i] = ordered


def copy_kernel(block, fan):
    for i in range(fan.shape[0]):
        fan[i] = block[...]


def fan_out(kernel, block, receivers):
    return pl.pallas_call(
        kernel,
        out_shape=jax.ShapeDtypeStruct((receivers,) + block.shape, jnp.bfloat16),
        in_specs=[pl.BlockSpec(memory_space=pltpu.VMEM)],
        out_specs=pl.BlockSpec(memory_space=pltpu.VMEM),
        compiler_params=pltpu.CompilerParams(vmem_limit_bytes=VMEM_LIMIT),
    )(block)


def middle_kernel(
    keep_row, group, w_gate, w_up, w_down, term, hidden, gate_grad, up_grad, sums, both
):
    blocks, pair, width = group.shape
    half = pair // 2
    size = blocks * half
    units = w_gate.shape[1]
    sums[...] = jnp.zeros_like(sums)

    def forward(i, carry):
        part = pl.ds(pl.multiple_of(i * STEP, STEP), STEP)
        rows = group[:, :half, part].reshape(size, STEP)
        cots = group[:, half:, part].reshape(size, STEP)
        weights = jnp.concatenate((w_gate[part, :], w_up[part, :]), axis=1)
        sums[:, : 2 * units] += dot(rows, weights)
        sums[:, 2 * units :] += dot(cots, w_down[:, part], NT)
        return carry

    lax.fori_loop(0, width // STEP, forward, 0, unroll=True)
    keep = keep_row[0:1, :]
    gate, up, hidden_grad = sums[:, :units], sums[:, units : 2 * units], sums[:, 2 * units :]
    sig = jax.nn.sigmoid(gate)
    act = gate * sig
    hidden[...] = (act * up * keep).astype(jnp.bfloat16)
    dup = (hidden_grad * act * keep).astype(jnp.bfloat16)
    dgate = (hidden_grad * up * sig * (1.0 + gate * (1.0 - sig)) * keep).astype(jnp.bfloat16)
    up_grad[...] = dup
    gate_grad[...] = dgate
    both[...] = jnp.concatenate((dgate, dup), axis=1)

    def backward(i, carry):
        part = pl.ds(pl.multiple_of(i * STEP, STEP), STEP)
        weights = jnp.concatenate((w_gate[part, :], w_up[part, :]), axis=1)
        out = dot(both[...], weights, NT).astype(jnp.bfloat16)
        term[:, :, part] = out.reshape(blocks, half, STEP)
        return carry

    lax.fori_loop(0, width // STEP, backward, 0, unroll=True)


def middle(keep, group, w_gate, w_up, w_down):
    blocks, pair, width = group.shape
    units = w_gate.shape[1]
    size = blocks * pair // 2
    vmem = pl.BlockSpec(memory_space=pltpu.VMEM)
    grads = jax.ShapeDtypeStruct((size, units), jnp.bfloat16)
    return pl.pallas_call(
        middle_kernel,
        out_shape=(
            jax.ShapeDtypeStruct((blocks, pair // 2, width), jnp.bfloat16),
            grads,
            grads,
            grads,
        ),
        in_specs=[vmem, vmem, vmem, vmem, vmem],
        out_specs=(vmem, vmem, vmem, vmem),
        scratch_shapes=[
            pltpu.VMEM((size, 3 * units), jnp.float32),
            pltpu.VMEM((size, 2 * units), jnp.bfloat16),
        ],
        compiler_params=pltpu.CompilerParams(vmem_limit_bytes=VMEM_LIMIT),
        cost_estimate=pl.CostEstimate(
            flops=10 * size * units * width, bytes_accessed=8 * 2**20, transcendentals=size * units
        ),
    )(keep, group, w_gate, w_up, w_down)


def sum_kernel(parts, out):
    def step(i, carry):
        part = pl.ds(pl.multiple_of(i * STEP, STEP), STEP)
        total = parts[0, :, part].astype(jnp.float32)
        for j in range(1, parts.shape[0]):
            total += parts[j, :, part].astype(jnp.float32)
        for j in range(out.shape[0]):
            out[j, :, part] = total[j * LIVE : (j + 1) * LIVE].astype(jnp.bfloat16)
        return carry

    lax.fori_loop(0, out.shape[2] // STEP, step, 0, unroll=True)


def sum_parts(parts):
    return pl.pallas_call(
        sum_kernel,
        out_shape=jax.ShapeDtypeStruct((4, LIVE, parts.shape[2]), jnp.bfloat16),
        in_specs=[pl.BlockSpec(memory_space=pltpu.VMEM)],
        out_specs=pl.BlockSpec(memory_space=pltpu.VMEM),
        compiler_params=pltpu.CompilerParams(vmem_limit_bytes=VMEM_LIMIT),
    )(parts)


def body(x_rows, cot_rows, counts, w_gate, w_up, w_down, kept_blocks, block_rank):
    experts, capacity, width = x_rows.shape[2:]
    my_expert = lax.axis_index(EXPERT)
    picked = jnp.arange(experts, dtype=jnp.int32)[None, :] == my_expert
    own_counts = jnp.sum(jnp.where(picked, counts[:, 0, :], 0), axis=1)
    chooser = compact_matrix(own_counts, capacity)
    back = chooser.reshape(LIVE, experts * capacity).T
    kind = jnp.eye(2, dtype=jnp.bfloat16)
    both = kind[:, None, None, :, None] * chooser[None, :, :, None, :]
    both = both.reshape(2 * LIVE, experts * 2 * capacity)

    slots = jnp.stack((x_rows[0, 0], cot_rows[0, 0]), axis=1)
    keep = (block_rank.reshape(()) < kept_blocks.reshape(())).astype(jnp.float32)
    keep = jnp.broadcast_to(keep, (8, w_gate.shape[2]))
    got = exchange(slots, EXPERT)
    got, both, back, keep = lax.optimization_barrier((got, both, back, keep))
    got = got.reshape(experts * 2 * capacity, width)
    packed = dot(both, got).astype(jnp.bfloat16)
    column = lax.all_gather(packed, "z_hi", axis=0, tiled=True)
    line = exchange(fan_out(order_kernel, column, 4), CHIP_PLANE, NEAR)
    group = exchange(fan_out(copy_kernel, line, 4), CHIP_PLANE, FAR)
    group = group.reshape(16, 8 * LIVE, width)
    term, hidden, gate_grad, up_grad = middle(
        keep, group, w_gate[0], w_up[0], w_down[0]
    )
    parts = exchange(term, CHIP_PLANE, WHOLE)
    plane_sum = sum_parts(parts)
    plane_sum, group, hidden, gate_grad, up_grad = lax.optimization_barrier(
        (plane_sum, group, hidden, gate_grad, up_grad)
    )
    parts = exchange(plane_sum, "z_hi")
    rows = group[:, : 4 * LIVE].reshape(64 * LIVE, width)
    cots = group[:, 4 * LIVE :].reshape(64 * LIVE, width)
    grad_down = dot(hidden, cots, TN).astype(jnp.bfloat16)
    grad_gate = dot(rows, gate_grad, TN).astype(jnp.bfloat16)
    grad_up = dot(rows, up_grad, TN).astype(jnp.bfloat16)
    parts, grad_gate, grad_up, grad_down = lax.optimization_barrier(
        (parts, grad_gate, grad_up, grad_down)
    )
    row_grads = jnp.sum(parts.astype(jnp.float32), axis=0).astype(jnp.bfloat16)
    slot_grads = dot(back, row_grads)
    slot_grads = slot_grads.astype(jnp.bfloat16).reshape(experts, capacity, width)
    grad_rows = exchange(slot_grads, EXPERT)[None, None]
    return (grad_rows, grad_gate[None], grad_up[None], grad_down[None])


def solution(mesh):
    fine = Mesh(np.asarray(mesh.devices).reshape(4, 2, 4, 4, 4), EXPERT + DP)
    in_specs = (
        P(EXPERT, DP, None, None, None),
        P(EXPERT, DP, None, None, None),
        P(None, DP, None),
        P(EXPERT, None, DP),
        P(EXPERT, None, DP),
        P(EXPERT, DP, None),
        P(EXPERT),
        P(EXPERT, DP),
    )
    out_specs = (
        P(EXPERT, DP, None, None, None),
        P(EXPERT, None, DP),
        P(EXPERT, None, DP),
        P(EXPERT, DP, None),
    )
    return jax.shard_map(body, mesh=fine, in_specs=in_specs, out_specs=out_specs, check_vma=False)
```

```python
import jax
import jax.numpy as jnp
import numpy as np
from jax import lax
from jax.experimental import pallas as pl
from jax.experimental.pallas import tpu as pltpu
from jax.sharding import Mesh
from jax.sharding import PartitionSpec as P

LIVE = 4
EXPERT = ("z_lo", "core")
DP = ("z_hi", "x", "y")
STEP = 512
NN = (((1,), (0,)), ((), ()))
NT = (((1,), (1,)), ((), ()))
TN = (((0,), (0,)), ((), ()))
VMEM_LIMIT = 40 * 2**20


def dot(left, right, dims=NN):
    return lax.dot_general(left, right, dims, preferred_element_type=jnp.float32)


def compact_matrix(slot_counts, capacity):
    sources = slot_counts.shape[0]
    earlier = jnp.arange(sources)[None, :] < jnp.arange(sources)[:, None]
    offsets = jnp.sum(jnp.where(earlier, slot_counts[None, :], 0), axis=1)
    within = jnp.arange(capacity, dtype=jnp.int32)[None, :]
    target = jnp.where(within < slot_counts[:, None], offsets[:, None] + within, -1)
    row = jnp.arange(LIVE, dtype=jnp.int32)[:, None, None]
    return (row == target[None]).astype(jnp.bfloat16)


CHIP_PLANE = ("core", "x", "y")
ALONG_X = [[x * 4 + y for x in range(4)] for y in range(4)]
ALONG_Y = [[x * 4 + y for y in range(4)] for x in range(4)]


def per_core(first, second):
    return first + [[16 + place for place in group] for group in second]


NEAR = per_core(ALONG_Y, ALONG_X)
FAR = per_core(ALONG_X, ALONG_Y)
WHOLE = per_core([sum(ALONG_Y, [])], [sum(ALONG_X, [])])


def exchange(array, axes, groups=None):
    return lax.all_to_all(
        array, axes, split_axis=0, concat_axis=0, axis_index_groups=groups, tiled=True
    )


def pair_kernel(rows, cots, pairs):
    pairs[:, 0] = rows[...]
    pairs[:, 1] = cots[...]


def pair_up(rows, cots):
    vmem = pl.BlockSpec(memory_space=pltpu.VMEM)
    return pl.pallas_call(
        pair_kernel,
        out_shape=jax.ShapeDtypeStruct((rows.shape[0], 2) + rows.shape[1:], jnp.bfloat16),
        in_specs=[vmem, vmem],
        out_specs=vmem,
    )(rows, cots)


def order_kernel(column, fan):
    size = column.shape[0]
    out = lax.broadcasted_iota(jnp.int32, (size, size), 0)
    source = ((out & 15) >> 2) * 8 + (out >> 4) * 4 + (out & 3)
    order = (source == lax.broadcasted_iota(jnp.int32, (size, size), 1)).astype(jnp.bfloat16)
    ordered = dot(order, column[...]).astype(jnp.bfloat16)
    for i in range(fan.shape[0]):
        fan[i] = ordered


def copy_kernel(block, fan):
    for i in range(fan.shape[0]):
        fan[i] = block[...]


def fan_out(kernel, block, receivers):
    return pl.pallas_call(
        kernel,
        out_shape=jax.ShapeDtypeStruct((receivers,) + block.shape, jnp.bfloat16),
        in_specs=[pl.BlockSpec(memory_space=pltpu.VMEM)],
        out_specs=pl.BlockSpec(memory_space=pltpu.VMEM),
        compiler_params=pltpu.CompilerParams(vmem_limit_bytes=VMEM_LIMIT),
    )(block)


def middle_kernel(
    keep_row, group, w_gate, w_up, w_down, term, hidden, gate_grad, up_grad, sums, both
):
    blocks, pair, width = group.shape
    half = pair // 2
    size = blocks * half
    units = w_gate.shape[1]
    sums[...] = jnp.zeros_like(sums)

    def forward(i, carry):
        part = pl.ds(pl.multiple_of(i * STEP, STEP), STEP)
        rows = group[:, :half, part].reshape(size, STEP)
        cots = group[:, half:, part].reshape(size, STEP)
        weights = jnp.concatenate((w_gate[part, :], w_up[part, :]), axis=1)
        sums[:, : 2 * units] += dot(rows, weights)
        sums[:, 2 * units :] += dot(cots, w_down[:, part], NT)
        return carry

    lax.fori_loop(0, width // STEP, forward, 0, unroll=True)
    keep = keep_row[0:1, :]
    gate, up, hidden_grad = sums[:, :units], sums[:, units : 2 * units], sums[:, 2 * units :]
    sig = jax.nn.sigmoid(gate)
    act = gate * sig
    hidden[...] = (act * up * keep).astype(jnp.bfloat16)
    dup = (hidden_grad * act * keep).astype(jnp.bfloat16)
    dgate = (hidden_grad * up * sig * (1.0 + gate * (1.0 - sig)) * keep).astype(jnp.bfloat16)
    up_grad[...] = dup
    gate_grad[...] = dgate
    both[...] = jnp.concatenate((dgate, dup), axis=1)

    def backward(i, carry):
        part = pl.ds(pl.multiple_of(i * STEP, STEP), STEP)
        weights = jnp.concatenate((w_gate[part, :], w_up[part, :]), axis=1)
        out = dot(both[...], weights, NT).astype(jnp.bfloat16)
        term[:, :, part] = out.reshape(blocks, half, STEP)
        return carry

    lax.fori_loop(0, width // STEP, backward, 0, unroll=True)


def middle(keep, group, w_gate, w_up, w_down):
    blocks, pair, width = group.shape
    units = w_gate.shape[1]
    size = blocks * pair // 2
    vmem = pl.BlockSpec(memory_space=pltpu.VMEM)
    grads = jax.ShapeDtypeStruct((size, units), jnp.bfloat16)
    return pl.pallas_call(
        middle_kernel,
        out_shape=(
            jax.ShapeDtypeStruct((blocks, pair // 2, width), jnp.bfloat16),
            grads,
            grads,
            grads,
        ),
        in_specs=[vmem, vmem, vmem, vmem, vmem],
        out_specs=(vmem, vmem, vmem, vmem),
        scratch_shapes=[
            pltpu.VMEM((size, 3 * units), jnp.float32),
            pltpu.VMEM((size, 2 * units), jnp.bfloat16),
        ],
        compiler_params=pltpu.CompilerParams(vmem_limit_bytes=VMEM_LIMIT),
        cost_estimate=pl.CostEstimate(
            flops=10 * size * units * width, bytes_accessed=8 * 2**20, transcendentals=size * units
        ),
    )(keep, group, w_gate, w_up, w_down)


def sum_kernel(parts, out):
    def step(i, carry):
        part = pl.ds(pl.multiple_of(i * STEP, STEP), STEP)
        total = parts[0, :, part].astype(jnp.float32)
        for j in range(1, parts.shape[0]):
            total += parts[j, :, part].astype(jnp.float32)
        for j in range(out.shape[0]):
            out[j, :, part] = total[j * LIVE : (j + 1) * LIVE].astype(jnp.bfloat16)
        return carry

    lax.fori_loop(0, out.shape[2] // STEP, step, 0, unroll=True)


def sum_parts(parts):
    return pl.pallas_call(
        sum_kernel,
        out_shape=jax.ShapeDtypeStruct((4, LIVE, parts.shape[2]), jnp.bfloat16),
        in_specs=[pl.BlockSpec(memory_space=pltpu.VMEM)],
        out_specs=pl.BlockSpec(memory_space=pltpu.VMEM),
        compiler_params=pltpu.CompilerParams(vmem_limit_bytes=VMEM_LIMIT),
    )(parts)


def body(x_rows, cot_rows, counts, w_gate, w_up, w_down, kept_blocks, block_rank):
    experts, capacity, width = x_rows.shape[2:]
    my_expert = lax.axis_index(EXPERT)
    picked = jnp.arange(experts, dtype=jnp.int32)[None, :] == my_expert
    own_counts = jnp.sum(jnp.where(picked, counts[:, 0, :], 0), axis=1)
    chooser = compact_matrix(own_counts, capacity)
    back = chooser.reshape(LIVE, experts * capacity).T
    kind = jnp.eye(2, dtype=jnp.bfloat16)
    both = kind[:, None, None, :, None] * chooser[None, :, :, None, :]
    both = both.reshape(2 * LIVE, experts * 2 * capacity)

    slots = pair_up(x_rows[0, 0], cot_rows[0, 0])
    keep = (block_rank.reshape(()) < kept_blocks.reshape(())).astype(jnp.float32)
    keep = jnp.broadcast_to(keep, (8, w_gate.shape[2]))
    got = exchange(slots, EXPERT)
    got, both, back, keep = lax.optimization_barrier((got, both, back, keep))
    got = got.reshape(experts * 2 * capacity, width)
    packed = dot(both, got).astype(jnp.bfloat16)
    column = lax.all_gather(packed, "z_hi", axis=0, tiled=True)
    line = exchange(fan_out(order_kernel, column, 4), CHIP_PLANE, NEAR)
    group = exchange(fan_out(copy_kernel, line, 4), CHIP_PLANE, FAR)
    group = group.reshape(16, 8 * LIVE, width)
    term, hidden, gate_grad, up_grad = middle(
        keep, group, w_gate[0], w_up[0], w_down[0]
    )
    parts = exchange(term, CHIP_PLANE, WHOLE)
    plane_sum = sum_parts(parts)
    plane_sum, group, hidden, gate_grad, up_grad = lax.optimization_barrier(
        (plane_sum, group, hidden, gate_grad, up_grad)
    )
    parts = exchange(plane_sum, "z_hi")
    rows = group[:, : 4 * LIVE].reshape(64 * LIVE, width)
    cots = group[:, 4 * LIVE :].reshape(64 * LIVE, width)
    grad_down = dot(hidden, cots, TN).astype(jnp.bfloat16)
    grad_gate = dot(rows, gate_grad, TN).astype(jnp.bfloat16)
    grad_up = dot(rows, up_grad, TN).astype(jnp.bfloat16)
    parts, grad_gate, grad_up, grad_down = lax.optimization_barrier(
        (parts, grad_gate, grad_up, grad_down)
    )
    row_grads = jnp.sum(parts.astype(jnp.float32), axis=0).astype(jnp.bfloat16)
    slot_grads = dot(back, row_grads)
    slot_grads = slot_grads.astype(jnp.bfloat16).reshape(experts, capacity, width)
    grad_rows = exchange(slot_grads, EXPERT)[None, None]
    return (grad_rows, grad_gate[None], grad_up[None], grad_down[None])


def solution(mesh):
    fine = Mesh(np.asarray(mesh.devices).reshape(4, 2, 4, 4, 4), EXPERT + DP)
    in_specs = (
        P(EXPERT, DP, None, None, None),
        P(EXPERT, DP, None, None, None),
        P(None, DP, None),
        P(EXPERT, None, DP),
        P(EXPERT, None, DP),
        P(EXPERT, DP, None),
        P(EXPERT),
        P(EXPERT, DP),
    )
    out_specs = (
        P(EXPERT, DP, None, None, None),
        P(EXPERT, None, DP),
        P(EXPERT, None, DP),
        P(EXPERT, DP, None),
    )
    return jax.shard_map(body, mesh=fine, in_specs=in_specs, out_specs=out_specs, check_vma=False)
```
